512 devices in a mesh: prompt: 2 (over y_lo), seq: 32 (over x, z), resp: 8 (over y_hi, core).
Axes of the slice: x: 4, y: 8 (y_hi: 4, y_lo: 2; y = y_hi * 2 + y_lo), z: 8, core: 2. Of those that a mesh axis runs over, the one named last changes fastest.
Arguments:
- prompt_queries: bfloat16 [8192, 8192], P(('prompt', 'seq', 'resp')), parts along dimension 0, may hold values from -20 to 20
- prompt_keys: bfloat16 [8192, 1024], P(('prompt', 'seq', 'resp')), parts along dimension 0, may hold values from -20 to 20
- prompt_values: bfloat16 [8192, 1024], P(('prompt', 'seq', 'resp')), parts along dimension 0, may hold values from -6 to 6
- answer_queries: bfloat16 [16384, 8192], P(('prompt', 'seq', 'resp')), parts along dimension 0, may hold values from -20 to 20
- answer_keys: bfloat16 [16384, 1024], P(('prompt', 'seq', 'resp')), parts along dimension 0, may hold values from -20 to 20
- answer_values: bfloat16 [16384, 1024], P(('prompt', 'seq', 'resp')), parts along dimension 0, may hold values from -6 to 6
- answer_lengths: int32 [32], P('prompt'), parts along dimension 0, may hold values from 1 to 512, 6144 in all
Outputs:
- prompt_attended: bfloat16 [8192, 8192], P(('prompt', 'seq', 'resp')), parts along dimension 0
- answer_attended: bfloat16 [16384, 8192], P(('prompt', 'seq', 'resp')), parts along dimension 0
The draws below stay inside these ranges and needn't reach their ends.
There are 2 independent parts, one for each index of `prompt`. The reference program is written for one: setup_inputs(seed, part) draws one part's arguments, and reference() takes and returns one part's arrays. A program takes and returns all parts, laid end to end along the dimension named above; each array names one. Nothing has to cross between parts.
Inputs may be any that keep to these rules, and one draw needn't show every extreme that they name: `answer_lengths`: the lengths sum to 6144 and the longest is exactly 512.
All inputs are finite; a program needn't handle non-finite values.
Results may differ from the reference program's by a relative error of at most 0.008.
Values may be sent and summed in bfloat16 or wider, within the bound.
A program may use at most 64 MiB of HBM per device.

```python
import math
import jax
import jax.numpy as jnp
import numpy as np
from jax import lax

H = 64
KVH = 8
DH = 128
RLEN = 512
P_SIZE = 4096
NRESP = 16


def normal_rows(key, height, breadth, factor):
    return factor * jnp.clip(jax.random.normal(key, (height, breadth), jnp.float32), -6.0, 6.0)


def draw_prompt_keys(key, part):
    key = jax.random.fold_in(key, 11)
    matrix = normal_rows(key, P_SIZE, KVH * DH, 1.0)
    return matrix.astype(jnp.bfloat16)


def draw_prompt_queries(key, part):
    key = jax.random.fold_in(key, 12)
    matrix = normal_rows(key, P_SIZE, H * DH, 1.5)
    return matrix.astype(jnp.bfloat16)


def draw_answer_queries(key, part):
    key = jax.random.fold_in(key, 13)
    matrix = normal_rows(key, NRESP * RLEN, H * DH, 1.5)
    return matrix.astype(jnp.bfloat16)


def draw_answer_keys(key, part):
    key = jax.random.fold_in(key, 14)
    matrix = normal_rows(key, NRESP * RLEN, KVH * DH, 1.0)
    return matrix.astype(jnp.bfloat16)


def shard_levels(key, extent, cuts, least, top_value):
    def one(position, blocks):
        steps = jax.random.uniform(jax.random.fold_in(jax.random.fold_in(key, 6), position), (blocks,), jnp.float32, least / len(cuts), top_value / len(cuts))
        return jnp.repeat(jnp.exp(steps), extent[position] // blocks).reshape((-1,) + (1,) * (len(extent) - position - 1))

    gain = one(*cuts[0])
    for cut in cuts[1:]:
        gain = gain * one(*cut)
    return gain


def length_profile(count, total, limit, lean):
    loads = [(1 << 20) // math.isqrt(standing ** lean) + 1 for standing in range(2, count + 1)]
    rest, given = total - limit - (count - 1), [1] * (count - 1)
    while rest > 0:
        candidates = [i for i in range(count - 1) if given[i] < limit]
        pool, left = sum([loads[i] for i in candidates]), rest
        for i in candidates:
            addition = min(limit - given[i], max(1, left * loads[i] // pool), rest)
            given[i] = given[i] + addition
            rest = rest - addition
    return np.array([limit] + given)


def uneven(key, count, total, most, slope):
    if count == 2:
        one = jax.random.randint(key, (), max(1, total - most), min(most, total - 1) + 1)
        return jnp.stack([one, total - one])
    lengths = jnp.asarray(length_profile(count, total, most, slope), jnp.int32)
    twos = (count - 1) // 2
    donor, sink = lengths[1:1 + 2 * twos:2], lengths[2:2 + 2 * twos:2]
    margin = jnp.minimum(donor - 1, most - sink)
    moved = jax.random.randint(jax.random.fold_in(key, 1), (twos,), 0, 1 << 20) % (margin + 1)
    lengths = lengths.at[1:1 + 2 * twos:2].set(donor - moved).at[2:2 + 2 * twos:2].set(sink + moved)
    return lengths[jax.random.permutation(jax.random.fold_in(key, 2), count)]


def scatter_about(key, shape, scale, reach, shards=(), kind=jnp.bfloat16):
    loudness = shard_levels(key, shape, shards, -0.22, 0.18) if shards else 1.0
    values = jax.random.normal(key, shape, jnp.float32) * scale * loudness
    return jnp.minimum(jnp.maximum(values, -reach), reach).astype(kind)


def setup_inputs(seed: int = 0, part: int = 0) -> dict:
    splits = jax.random.split(jax.random.key(seed), 8)
    own_keys = jax.random.split(jax.random.fold_in(splits[7], part), 8)
    prompt_queries = draw_prompt_queries(jax.random.fold_in(jax.random.fold_in(splits[7], part), 71), part)
    prompt_keys = draw_prompt_keys(jax.random.fold_in(jax.random.fold_in(splits[7], part), 71), part)
    prompt_values = scatter_about(own_keys[2], (P_SIZE, KVH * DH), 1.0, 6.0, ((0, 256),))
    answer_queries = draw_answer_queries(jax.random.fold_in(jax.random.fold_in(splits[7], part), 71), part)
    answer_keys = draw_answer_keys(jax.random.fold_in(jax.random.fold_in(splits[7], part), 71), part)
    answer_values = scatter_about(own_keys[5], (NRESP * RLEN, KVH * DH), 1.0, 6.0, ((0, 256),))
    answer_lengths = uneven(own_keys[6], NRESP, 3 * NRESP * RLEN // 4, RLEN, 1).astype(jnp.int32)
    return {"prompt_queries": prompt_queries, "prompt_keys": prompt_keys, "prompt_values": prompt_values, "answer_queries": answer_queries, "answer_keys": answer_keys, "answer_values": answer_values, "answer_lengths": answer_lengths}


def reference(prompt_queries, prompt_keys, prompt_values, answer_queries, answer_keys, answer_values, answer_lengths):
    group_size = H // KVH
    score_scale = 1.0 / math.sqrt(DH)
    prompt_places = jnp.arange(P_SIZE, dtype=jnp.int32)
    causal = prompt_places[None, :] <= prompt_places[:, None]
    answer_places = jnp.arange(RLEN, dtype=jnp.int32)
    answer_causal = answer_places[None, :] <= answer_places[:, None]
    live_rows = (answer_places[None, :] < answer_lengths[:, None]).reshape(NRESP * RLEN, 1)

    def one_head(head_index):
        shared_head = head_index // group_size
        query = lax.dynamic_slice_in_dim(prompt_queries, head_index * DH, DH, 1)
        keys = lax.dynamic_slice_in_dim(prompt_keys, shared_head * DH, DH, 1)
        values = lax.dynamic_slice_in_dim(prompt_values, shared_head * DH, DH, 1)
        scores = jnp.dot(query, keys.T, preferred_element_type=jnp.float32) * score_scale
        scores = jnp.where(causal, scores, -jnp.inf)
        weights = jnp.exp(scores - lax.optimization_barrier(jnp.max(scores, axis=1, keepdims=True)))
        summed = jnp.dot(weights.astype(jnp.bfloat16), values, preferred_element_type=jnp.float32)
        prompt_head = (summed / lax.optimization_barrier(jnp.sum(weights, axis=1, keepdims=True))).astype(jnp.bfloat16)
        answer_query = lax.dynamic_slice_in_dim(answer_queries, head_index * DH, DH, 1)
        answer_key = lax.dynamic_slice_in_dim(answer_keys, shared_head * DH, DH, 1)
        answer_value = lax.dynamic_slice_in_dim(answer_values, shared_head * DH, DH, 1)
        cross = jnp.dot(answer_query, keys.T, preferred_element_type=jnp.float32) * score_scale
        query_three = answer_query.astype(jnp.float32).reshape(NRESP, RLEN, DH)
        key_three = answer_key.astype(jnp.float32).reshape(NRESP, RLEN, DH)
        value_three = answer_value.astype(jnp.float32).reshape(NRESP, RLEN, DH)
        own = jnp.einsum('nqd,nkd->nqk', query_three, key_three, precision=lax.Precision.HIGHEST) * score_scale
        own = jnp.where(answer_causal[None, :, :], own, -jnp.inf)
        top_score = jnp.maximum(lax.optimization_barrier(jnp.max(cross, axis=1)).reshape(NRESP, RLEN), lax.optimization_barrier(jnp.max(own, axis=2)))
        cross_weights = jnp.exp(cross - top_score.reshape(NRESP * RLEN, 1))
        own_weights = jnp.exp(own - top_score[:, :, None])
        totals = lax.optimization_barrier(jnp.sum(cross_weights, axis=1)).reshape(NRESP, RLEN) + lax.optimization_barrier(jnp.sum(own_weights, axis=2))
        rounded = lax.optimization_barrier(own_weights.astype(jnp.bfloat16))
        gathered = jnp.dot(cross_weights.astype(jnp.bfloat16), values, preferred_element_type=jnp.float32).reshape(NRESP, RLEN, DH)
        gathered = gathered + jnp.einsum('nqk,nkd->nqd', rounded.astype(jnp.float32), value_three, precision=lax.Precision.HIGHEST)
        answer_head = (gathered / totals[:, :, None]).reshape(NRESP * RLEN, DH)
        answer_head = jnp.where(live_rows, answer_head, 0.0).astype(jnp.bfloat16)
        return (prompt_head, answer_head)
    prompt_heads, answer_heads = lax.map(one_head, jnp.arange(H, dtype=jnp.int32))
    prompt_attended = jnp.transpose(prompt_heads, (1, 0, 2)).reshape(P_SIZE, H * DH)
    answer_attended = jnp.transpose(answer_heads, (1, 0, 2)).reshape(NRESP * RLEN, H * DH)
    return (prompt_attended, answer_attended)
```

```python
import math

import jax
import jax.numpy as jnp
from jax import lax
from jax.experimental import pallas as pl
from jax.experimental.pallas import tpu as pltpu
from jax.sharding import PartitionSpec as P

DH = 128
ZN = 8
SCALE = math.log2(math.e) / math.sqrt(DH)
BIG_NEG = -1e30
MESH = pl.DeviceIdType.MESH

(R_KV, R_AKV, R_QP, R_QA, R_X, R_OP, R_OA, R_KZL, R_KZR, R_KZ2, R_KYL, R_KYR, R_KY2,
 R_VYL, R_VYR, R_VY2, R_VZL, R_VZR, R_VZ2, R_AL, R_AR, R_A2) = range(22)
N_RECV = 22
N_SEND = 80


def dot_t(a, b):
    return lax.dot_general(a, b, (((1,), (1,)), ((), ())), preferred_element_type=jnp.float32)


def attend(q, pieces, state):
    scores = []
    for keys, values, mask in pieces:
        s = dot_t(q, keys())
        if mask is not None:
            s = jnp.where(mask, s, BIG_NEG)
        scores.append(s)
    top = None
    for s in scores:
        t = jnp.max(s, axis=1, keepdims=True)
        top = t if top is None else jnp.maximum(top, t)
    if state is not None:
        old_top, old_total, old_sum = state
        top = jnp.maximum(top, old_top)
    total, acc = None, None
    for s, (keys, values, mask) in zip(scores, pieces):
        p = jnp.exp2((s - top) * SCALE)
        row = jnp.sum(p, axis=1, keepdims=True)
        part = jnp.dot(p.astype(jnp.bfloat16), values(), preferred_element_type=jnp.float32)
        total = row if total is None else total + row
        acc = part if acc is None else acc + part
    if state is not None:
        rescale = jnp.exp2((old_top - top) * SCALE)
        total = total + old_total * rescale
        acc = acc + old_sum * rescale
    return top, total, acc


def kernel(pq, pk, pv, aq, ak, av, po, ao, kv, akv, qp, qa, op, oa, accs, tops, totals,
           send_sems, pout_sems, aout_sems, recv_sems):
    part = lax.axis_index("prompt")
    seq = lax.axis_index("seq")
    resp = lax.axis_index("resp")
    x, z = seq // ZN, seq % ZN
    y, core = resp // 2, resp % 2
    xb = x // 2
    xp = xb * (3 - x) + (1 - xb) * x
    zh, zb = z // 2, z % 2
    me = xb * 4 + zb * 2 + core

    def place(xx, zz, yy, cc):
        return (part, xx * ZN + zz, yy * 2 + cc)

    def member(dx, dz, dc):
        xb2, zb2, c2 = (xb + dx) % 2, (zb + dz) % 2, (core + dc) % 2
        x2 = xb2 * (3 - xp) + (1 - xb2) * xp
        return xb2 * 4 + zb2 * 2 + c2, place(x2, zh * 2 + zb2, y, c2)

    def around(v, d):
        return (v + d + 4) % 4

    def z_dev(d):
        return place(x, around(zh, d) * 2 + zb, y, core)

    def y_dev(d):
        return place(x, z, around(y, d), core)

    x_dev = place(xb * (2 + xp) + (1 - xb) * (1 - xp), z, y, core)
    xq = 1 - xp

    peers = [member(d // 4, (d // 2) % 2, d % 2) for d in range(8)]
    partners = [p[1] for p in peers[1:]] + [z_dev(1), z_dev(-1), y_dev(1), y_dev(-1), x_dev]

    barrier = pltpu.get_barrier_semaphore()
    for dev in partners:
        pl.semaphore_signal(barrier, inc=1, device_id=dev, device_id_type=MESH)

    def heads(ref, h, width):
        return ref.at[:, pl.ds(pl.multiple_of(h * width, width), width)]

    rows_p = pl.ds(pl.multiple_of(core * 16, 16), 16)
    rows_a = pl.ds(pl.multiple_of(core * 32, 32), 32)
    k_land, v_land = kv.at[0, xb, xp, zh, zb, y, rows_p], kv.at[1, xb, xp, zh, zb, y, rows_p]
    ak_land, av_land = akv.at[0, xb, zb, y, rows_a], akv.at[1, xb, zb, y, rows_a]

    for src, dst, r in (
        (heads(pk, me, DH), k_land, R_KV),
        (heads(pv, me, DH), v_land, R_KV),
        (heads(ak, me, DH), ak_land, R_AKV),
        (heads(av, me, DH), av_land, R_AKV),
        (heads(pq, me, 8 * DH), qp.at[me], R_QP),
        (heads(aq, me, 8 * DH), qa.at[me], R_QA),
    ):
        pltpu.make_async_copy(src, dst, recv_sems.at[r]).start()

    pl.semaphore_wait(barrier, len(partners))

    sends = []

    def send(src, dst, r, dev):
        copy = pltpu.make_async_remote_copy(
            src_ref=src, dst_ref=dst, send_sem=send_sems.at[len(sends)],
            recv_sem=recv_sems.at[r], device_id=dev, device_id_type=MESH)
        copy.start()
        sends.append(copy)

    def pass_on(ref, r, dev):
        send(ref, ref, r, dev)

    def arrived(ref, r):
        pltpu.make_async_copy(ref, ref, recv_sems.at[r]).wait()

    order = (7, 6, 5, 4, 3, 2, 1)
    for d in order:
        h, dev = peers[d]
        send(heads(pk, h, DH), k_land, R_KV, dev)
        send(heads(pv, h, DH), v_land, R_KV, dev)
    for d in order:
        h, dev = peers[d]
        send(heads(ak, h, DH), ak_land, R_AKV, dev)
        send(heads(av, h, DH), av_land, R_AKV, dev)

    def shard(n, dz, dy):
        return kv.at[n, :, xp, around(zh, dz), :, around(y, dy)]

    def half(n, b, dz, dy):
        return kv.at[n, b, xp, around(zh, dz), :, around(y, dy)]

    def k_plane(dy):
        return kv.at[0, :, xp, :, :, around(y, dy)]

    def v_plane(dz):
        return kv.at[1, :, xp, around(zh, dz)]

    arrived(kv.at[:, :, xp, zh, :, y], R_KV)
    pass_on(shard(0, 0, 0), R_KZL, z_dev(1))
    pass_on(shard(0, 0, 0), R_KZR, z_dev(-1))
    pass_on(shard(1, 0, 0), R_VYL, y_dev(1))
    pass_on(shard(1, 0, 0), R_VYR, y_dev(-1))
    pass_on(shard(0, 0, 0), R_X, x_dev)
    pass_on(shard(1, 0, 0), R_X, x_dev)
    for d in order:
        h, dev = peers[d]
        send(heads(pq, h, 8 * DH), qp.at[me], R_QP, dev)
    for d in order:
        h, dev = peers[d]
        send(heads(aq, h, 8 * DH), qa.at[me], R_QA, dev)
    arrived(shard(0, -1, 0), R_KZL)
    pass_on(half(0, 0, -1, 0), R_KZ2, z_dev(1))
    arrived(shard(0, 1, 0), R_KZR)
    pass_on(half(0, 1, 1, 0), R_KZ2, z_dev(-1))
    arrived(shard(1, 0, -1), R_VYL)
    pass_on(half(1, 0, 0, -1), R_VY2, y_dev(1))
    arrived(shard(1, 0, 1), R_VYR)
    pass_on(half(1, 1, 0, 1), R_VY2, y_dev(-1))
    pass_on(shard(0, -1, 0), R_X, x_dev)
    pass_on(shard(0, 1, 0), R_X, x_dev)
    pass_on(shard(1, 0, -1), R_X, x_dev)
    pass_on(shard(1, 0, 1), R_X, x_dev)
    arrived(shard(0, 2, 0), R_KZ2)
    pass_on(k_plane(0), R_KYL, y_dev(1))
    pass_on(k_plane(0), R_KYR, y_dev(-1))
    arrived(shard(1, 0, 2), R_VY2)
    pass_on(v_plane(0), R_VZL, z_dev(1))
    pass_on(v_plane(0), R_VZR, z_dev(-1))
    pass_on(shard(0, 2, 0), R_X, x_dev)
    pass_on(shard(1, 0, 2), R_X, x_dev)
    arrived(akv.at[:, :, :, y], R_AKV)
    pass_on(akv.at[:, :, :, y], R_AL, y_dev(1))
    pass_on(akv.at[:, :, :, y], R_AR, y_dev(-1))
    arrived(k_plane(-1), R_KYL)
    pass_on(kv.at[0, 0, xp, :, :, around(y, -1)], R_KY2, y_dev(1))
    arrived(k_plane(1), R_KYR)
    pass_on(kv.at[0, 1, xp, :, :, around(y, 1)], R_KY2, y_dev(-1))
    arrived(v_plane(-1), R_VZL)
    pass_on(kv.at[1, 0, xp, around(zh, -1)], R_VZ2, z_dev(1))
    arrived(v_plane(1), R_VZR)
    pass_on(kv.at[1, 1, xp, around(zh, 1)], R_VZ2, z_dev(-1))
    pass_on(k_plane(-1), R_X, x_dev)
    pass_on(v_plane(-1), R_X, x_dev)
    pass_on(k_plane(1), R_X, x_dev)
    pass_on(v_plane(1), R_X, x_dev)
    arrived(akv.at[:, :, :, around(y, -1)], R_AL)
    pass_on(akv.at[0, :, :, around(y, -1)], R_A2, y_dev(1))
    arrived(akv.at[:, :, :, around(y, 1)], R_AR)
    pass_on(akv.at[1, :, :, around(y, 1)], R_A2, y_dev(-1))
    arrived(k_plane(2), R_KY2)
    pass_on(k_plane(2), R_X, x_dev)
    arrived(v_plane(2), R_VZ2)
    pass_on(v_plane(2), R_X, x_dev)

    def piece(b, xx, mask=None):
        return (
            lambda: kv[0, b, xx].reshape(1024, DH),
            lambda: kv[1, b, xx].reshape(1024, DH),
            mask,
        )

    def row_places(base, width):
        rows = lax.broadcasted_iota(jnp.int32, (256, width), 0)
        return (rows & 31) + base

    def key_places(width):
        return lax.broadcasted_iota(jnp.int32, (256, width), 1)

    def prompt_tile(t):
        cols = [slice(j * DH, (j + 1) * DH) for j in range(8)]
        return jnp.concatenate([qp[2 * t + c, :, s] for s in cols for c in range(2)], axis=0)

    def answer_tile(m):
        return jnp.concatenate([qa[m, :, j * DH:(j + 1) * DH] for j in range(8)], axis=0)

    def keep(t, state):
        top, total, acc = state
        tops[t] = jnp.broadcast_to(top, (256, DH))
        totals[t] = jnp.broadcast_to(total, (256, DH))
        accs[t] = acc

    def kept(t):
        return tops[t][:, :1], totals[t][:, :1], accs[t]

    arrived(qp, R_QP)

    def diagonal(zbq):
        return key_places(1024) <= row_places((2 * zh + zbq) * 128 + y * 32, 1024)

    @pl.loop(0, 2)
    def _(zbq):
        keep(8 + zbq, attend(prompt_tile(zbq), [piece(0, xp, diagonal(zbq))], None))
        keep(10 + zbq, attend(
            prompt_tile(2 + zbq), [piece(0, xp), piece(1, xp, diagonal(zbq))], None))

    arrived(qa, R_QA)

    @pl.loop(0, 8)
    def _(m):
        keep(m, attend(answer_tile(m), [piece(0, xp), piece(1, xp)], None))

    arrived(kv.at[:, :, xq], R_X)

    @pl.loop(0, 4)
    def _(u):
        zbq, v = u % 2, u // 2
        t = 2 * ((1 - xp) + xp * v) + zbq
        b = (1 - xp) * v
        keep(8 + t, attend(prompt_tile(t), [piece(b, xq)], kept(8 + t)))

    arrived(akv.at[:, :, :, around(y, 2)], R_A2)

    def pout(i, j):
        dx, dz = (3 - i) // 2, (3 - i) % 2
        m, dev = member(dx, dz, j)
        return m, dev

    @pl.loop(0, 4)
    def _(i):
        m0, _ignored = member((3 - i) // 2, (3 - i) % 2, 0)
        t = m0 // 2
        _top, total, acc = kept(8 + t)
        out = (acc / total).astype(jnp.bfloat16)
        for j in range(8):
            for c in range(2):
                r = j * 32 + c * 16
                op[2 * t + c, :, j * DH:(j + 1) * DH] = out[r:r + 16]
        m1, dev1 = member((3 - i) // 2, (3 - i) % 2, 1)
        pltpu.make_async_remote_copy(
            src_ref=op.at[m1], dst_ref=heads(po, me, 8 * DH), send_sem=pout_sems.at[2 * i],
            recv_sem=recv_sems.at[R_OP], device_id=dev1, device_id_type=MESH).start()

        @pl.when(i < 3)
        def _():
            m2, dev2 = member((3 - i) // 2, (3 - i) % 2, 0)
            pltpu.make_async_remote_copy(
                src_ref=op.at[m2], dst_ref=heads(po, me, 8 * DH),
                send_sem=pout_sems.at[2 * i + 1],
                recv_sem=recv_sems.at[R_OP], device_id=dev2, device_id_type=MESH).start()

        @pl.when(i == 3)
        def _():
            pltpu.make_async_copy(op.at[me], heads(po, me, 8 * DH), recv_sems.at[R_OP]).start()

    @pl.loop(0, 8)
    def _(i):
        d = 7 - i
        m, dev = member(d // 4, (d // 2) % 2, d % 2)
        a, h = m // 4, (m // 2) % 2
        mask = key_places(512) <= row_places(h * 256 + y * 64 + (m % 2) * 32, 512)
        own_piece = (
            lambda: akv[0, a].reshape(512, DH),
            lambda: akv[1, a].reshape(512, DH),
            mask,
        )
        _top, total, acc = attend(
            answer_tile(m), [piece(0, xq), piece(1, xq), own_piece], kept(m))
        out = (acc / total).astype(jnp.bfloat16)
        for j in range(8):
            oa[m, :, j * DH:(j + 1) * DH] = out[j * 32:(j + 1) * 32]

        @pl.when(i < 7)
        def _():
            pltpu.make_async_remote_copy(
                src_ref=oa.at[m], dst_ref=heads(ao, me, 8 * DH), send_sem=aout_sems.at[i],
                recv_sem=recv_sems.at[R_OA], device_id=dev, device_id_type=MESH).start()

        @pl.when(i == 7)
        def _():
            pltpu.make_async_copy(oa.at[me], heads(ao, me, 8 * DH), recv_sems.at[R_OA]).start()

    for copy in sends:
        copy.wait_send()
    for i in range(7):
        pltpu.make_async_copy(op.at[i], op.at[i], pout_sems.at[i]).wait()
        pltpu.make_async_copy(oa.at[i], oa.at[i], aout_sems.at[i]).wait()
    arrived(po, R_OP)
    arrived(ao, R_OA)


def shards(pq, pk, pv, aq, ak, av, answer_lengths):
    bf16, f32 = jnp.bfloat16, jnp.float32
    any_spec = pl.BlockSpec(memory_space=pl.ANY)
    prompt_out, answer_out = pl.pallas_call(
        kernel,
        out_shape=(
            jax.ShapeDtypeStruct(pq.shape, bf16),
            jax.ShapeDtypeStruct(aq.shape, bf16),
        ),
        in_specs=[any_spec] * 6,
        out_specs=(any_spec, any_spec),
        scratch_shapes=[
            pltpu.VMEM((2, 2, 2, 4, 2, 4, 32, DH), bf16),
            pltpu.VMEM((2, 2, 2, 4, 64, DH), bf16),
            pltpu.VMEM((8, 16, 8 * DH), bf16),
            pltpu.VMEM((8, 32, 8 * DH), bf16),
            pltpu.VMEM((8, 16, 8 * DH), bf16),
            pltpu.VMEM((8, 32, 8 * DH), bf16),
            pltpu.VMEM((12, 256, DH), f32),
            pltpu.VMEM((12, 256, DH), f32),
            pltpu.VMEM((12, 256, DH), f32),
            pltpu.SemaphoreType.DMA((N_SEND,)),
            pltpu.SemaphoreType.DMA((8,)),
            pltpu.SemaphoreType.DMA((8,)),
            pltpu.SemaphoreType.DMA((N_RECV,)),
        ],
        compiler_params=pltpu.CompilerParams(
            collective_id=0, has_side_effects=True, vmem_limit_bytes=48 * 1024 * 1024),
        cost_estimate=pl.CostEstimate(
            flops=6_400_000_000, bytes_accessed=2_000_000, transcendentals=12_000_000),
    )(pq, pk, pv, aq, ak, av)
    seq, resp = lax.axis_index("seq"), lax.axis_index("resp")
    height = aq.shape[0]
    places = (seq % 2) * 256 + resp * height + jnp.arange(height, dtype=jnp.int32)
    live = lax.dynamic_index_in_dim(answer_lengths, seq // 2, 0, keepdims=False)
    answer_out = jnp.where((places < live)[:, None], answer_out, jnp.zeros((), bf16))
    return prompt_out, answer_out


def solution(mesh):
    rows = P(("prompt", "seq", "resp"), None)
    return jax.shard_map(
        shards,
        mesh=mesh,
        in_specs=(rows,) * 6 + (P("prompt"),),
        out_specs=(rows, rows),
        check_vma=False,
    )
```

```python
import math

import jax
import jax.numpy as jnp
from jax import lax
from jax.experimental import pallas as pl
from jax.experimental.pallas import tpu as pltpu
from jax.sharding import PartitionSpec as P

DH = 128
ZN = 8
QW = 4 * DH
SCALE = math.log2(math.e) / math.sqrt(DH)
BIG_NEG = -1e30
MESH = pl.DeviceIdType.MESH

R_KV, R_AKV, R_QP, R_QA, R_OP, R_OA, R_A = 0, 1, 2, 3, 4, 5, 6
R_FIRST, R_SECOND, R_SIB, R_ASIB = 9, 12, 24, 40
N_RECV = 44
N_SEND = 112
DISTANCES = (0, -1, 1, 2)


def dot_t(a, b):
    return lax.dot_general(a, b, (((1,), (1,)), ((), ())), preferred_element_type=jnp.float32)


def attend(q, pieces, state):
    scores = []
    for keys, values, mask in pieces:
        s = dot_t(q, keys())
        if mask is not None:
            s = jnp.where(mask, s, BIG_NEG)
        scores.append(s)
    top = None
    for s in scores:
        t = jnp.max(s, axis=1, keepdims=True)
        top = t if top is None else jnp.maximum(top, t)
    if state is not None:
        old_top, old_total, old_sum = state
        top = jnp.maximum(top, old_top)
    total, acc = None, None
    for s, (keys, values, mask) in zip(scores, pieces):
        p = jnp.exp2((s - top) * SCALE)
        row = jnp.sum(p, axis=1, keepdims=True)
        part = jnp.dot(p.astype(jnp.bfloat16), values(), preferred_element_type=jnp.float32)
        total = row if total is None else total + row
        acc = part if acc is None else acc + part
    if state is not None:
        rescale = jnp.exp2((old_top - top) * SCALE)
        total = total + old_total * rescale
        acc = acc + old_sum * rescale
    return top, total, acc


def kernel(pq, pk, pv, aq, ak, av, po, ao, kv, akv, qp, qa, op, oa, accs, tops, totals,
           send_sems, pout_sems, aout_sems, recv_sems):
    part = lax.axis_index("prompt")
    seq = lax.axis_index("seq")
    resp = lax.axis_index("resp")
    x, z = seq // ZN, seq % ZN
    y, core = resp // 2, resp % 2
    zh, zb = z // 2, z % 2
    chip = x * 2 + zb
    me = chip * 2 + core
    mine, other = x // 2, 1 - core

    def place(xx, zz, yy, cc):
        return (part, xx * ZN + zz, yy * 2 + cc)

    def chip_at(dx, dz):
        x2, zb2 = (x + dx) % 4, (zb + dz) % 2
        return x2 * 2 + zb2, x2, zh * 2 + zb2

    def around(v, d):
        return (v + d + 4) % 4

    def first(d):
        return place(x, around(zh, (1 - core) * d) * 2 + zb, around(y, core * d), core)

    def second(d):
        return place(x, around(zh, core * d) * 2 + zb, around(y, (1 - core) * d), core)

    def y_dev(d):
        return place(x, z, around(y, d), core)

    sibling = place(x, z, y, other)
    chips = [chip_at(d // 2, d % 2) for d in range(8)]
    members = [
        (h * 2 + (core + dc) % 2, place(xx, zz, y, (core + dc) % 2))
        for h, xx, zz in chips for dc in range(2)
    ]
    partners = [dev for _, dev in members[1:]] + [first(1), first(-1), second(1), second(-1)]

    barrier = pltpu.get_barrier_semaphore()
    for dev in partners:
        pl.semaphore_signal(barrier, inc=1, device_id=dev, device_id_type=MESH)

    def cut(ref, h, width):
        return ref.at[:, pl.ds(pl.multiple_of(h * width, width), width)]

    rows_p = pl.ds(pl.multiple_of(core * 16, 16), 16)
    rows_a = pl.ds(pl.multiple_of(core * 32, 32), 32)
    k_land, v_land = kv.at[0, x, zh, zb, y, rows_p], kv.at[1, x, zh, zb, y, rows_p]
    ak_land, av_land = akv.at[0, x, zb, y, rows_a], akv.at[1, x, zb, y, rows_a]

    pltpu.make_async_copy(cut(pq, me, QW), qp.at[me], recv_sems.at[R_QP]).start()
    pltpu.make_async_copy(cut(aq, me, QW), qa.at[me], recv_sems.at[R_QA]).start()
    own_parts = (
        (cut(pk, chip, DH), k_land, R_KV), (cut(pv, chip, DH), v_land, R_KV),
        (cut(ak, chip, DH), ak_land, R_AKV), (cut(av, chip, DH), av_land, R_AKV))

    @pl.when(core == mine)
    def _():
        for src, dst, r in own_parts:
            pltpu.make_async_copy(src, dst, recv_sems.at[r]).start()

    pl.semaphore_wait(barrier, len(partners))

    sends = []

    def remote(src, dst, send_sem, r, dev):
        return pltpu.make_async_remote_copy(
            src_ref=src, dst_ref=dst, send_sem=send_sem,
            recv_sem=recv_sems.at[r], device_id=dev, device_id_type=MESH)

    def send(src, dst, r, dev):
        copy = remote(src, dst, send_sems.at[len(sends)], r, dev)
        copy.start()
        sends.append(copy)

    def pass_on(ref, r, dev):
        send(ref, ref, r, dev)

    def arrived(ref, r):
        pltpu.make_async_copy(ref, ref, recv_sems.at[r]).wait()

    own_sends = [remote(src, dst, aout_sems.at[16 + i], r, sibling)
                 for i, (src, dst, r) in enumerate(own_parts)]

    def part_of(c, d1, d2, n=slice(None)):
        zz = around(zh, (1 - c) * d1 + c * d2)
        yy = around(y, (1 - c) * d2 + c * d1)
        return kv.at[n, pl.ds(2 * c, 2), zz, :, yy]

    def shard(d1, d2):
        return part_of(core, d1, d2)

    def to_sibling(d1, d2):
        k = DISTANCES.index(d2) * 4 + DISTANCES.index(d1)
        pass_on(shard(d1, d2), R_SIB + k, sibling)

    def from_sibling(d1, d2):
        k = DISTANCES.index(d2) * 4 + DISTANCES.index(d1)
        arrived(part_of(other, d1, d2), R_SIB + k)

    def start_second(d1):
        r = R_SECOND + 3 * DISTANCES.index(d1)
        pass_on(shard(d1, 0), r, second(1))
        pass_on(shard(d1, 0), r + 1, second(-1))

    def middle_second(d1):
        r = R_SECOND + 3 * DISTANCES.index(d1)
        arrived(shard(d1, -1), r)
        pass_on(part_of(core, d1, -1, 0), r + 2, second(1))
        arrived(shard(d1, 1), r + 1)
        pass_on(part_of(core, d1, 1, 1), r + 2, second(-1))
        to_sibling(d1, -1)
        to_sibling(d1, 1)

    for d in (7, 6, 5, 4, 3, 2, 1):
        h, xx, zz = chips[d]
        send(cut(pk, h, DH), k_land, R_KV, place(xx, zz, y, mine))
        send(cut(pv, h, DH), v_land, R_KV, place(xx, zz, y, mine))

    @pl.when(core != mine)
    def _():
        for copy in own_sends:
            copy.start()

    arrived(shard(0, 0), R_KV)
    pass_on(shard(0, 0), R_FIRST, first(1))
    pass_on(shard(0, 0), R_FIRST + 1, first(-1))
    start_second(0)
    to_sibling(0, 0)
    for g, dev in members[:0:-1]:
        send(cut(aq, g, QW), qa.at[me], R_QA, dev)
    arrived(shard(-1, 0), R_FIRST)
    pass_on(part_of(core, -1, 0, 0), R_FIRST + 2, first(1))
    arrived(shard(1, 0), R_FIRST + 1)
    pass_on(part_of(core, 1, 0, 1), R_FIRST + 2, first(-1))
    start_second(-1)
    start_second(1)
    to_sibling(-1, 0)
    to_sibling(1, 0)
    for d in (7, 6, 5, 4, 3, 2, 1):
        h, xx, zz = chips[d]
        send(cut(ak, h, DH), ak_land, R_AKV, place(xx, zz, y, mine))
        send(cut(av, h, DH), av_land, R_AKV, place(xx, zz, y, mine))
    middle_second(0)
    arrived(shard(2, 0), R_FIRST + 2)
    start_second(2)
    to_sibling(2, 0)
    for g, dev in members[:0:-1]:
        send(cut(pq, g, QW), qp.at[me], R_QP, dev)

    def own_keys(c, dy, n=slice(None)):
        return akv.at[n, pl.ds(2 * c, 2), :, around(y, dy)]

    arrived(own_keys(core, 0), R_AKV)
    pass_on(own_keys(core, 0), R_A, y_dev(1))
    pass_on(own_keys(core, 0), R_A + 1, y_dev(-1))
    pass_on(own_keys(core, 0), R_ASIB, sibling)
    middle_second(-1)
    middle_second(1)
    middle_second(2)
    arrived(own_keys(core, -1), R_A)
    pass_on(own_keys(core, -1, 0), R_A + 2, y_dev(1))
    arrived(own_keys(core, 1), R_A + 1)
    pass_on(own_keys(core, 1, 1), R_A + 2, y_dev(-1))
    pass_on(own_keys(core, -1), R_ASIB + 1, sibling)
    pass_on(own_keys(core, 1), R_ASIB + 2, sibling)

    def low(dy):
        def take(n):
            return kv[n, 0:2, :, :, around(y, dy)].reshape(512, DH)
        return (lambda: take(0), lambda: take(1), None)

    def high(dz):
        def take(n):
            return kv[n, 2:4, around(zh, dz)].reshape(512, DH)
        return (lambda: take(0), lambda: take(1), None)

    def slab(xx, mask=None):
        return (lambda: kv[0, xx].reshape(1024, DH), lambda: kv[1, xx].reshape(1024, DH), mask)

    def iota(width, axis):
        return lax.broadcasted_iota(jnp.int32, (256, width), axis)

    def answer_tile(t):
        return jnp.concatenate(
            [qa[2 * t + c, :, j * DH:(j + 1) * DH] for j in range(4) for c in range(2)], axis=0)

    def prompt_tile(t):
        return jnp.concatenate(
            [qp[4 * t + c, :, j * DH:(j + 1) * DH] for j in range(4) for c in range(4)], axis=0)

    def keep(t, state):
        top, total, acc = state
        tops[t] = jnp.broadcast_to(top, (256, DH))
        totals[t] = jnp.broadcast_to(total, (256, DH))
        accs[t] = acc

    def kept(t):
        return tops[t][:, :1], totals[t][:, :1], accs[t]

    for d2 in (0, -1, 1):
        for d1 in DISTANCES:
            from_sibling(d1, d2)
    arrived(qa, R_QA)

    @pl.loop(0, 8)
    def _(t):
        keep(t, attend(answer_tile(t), [f(d) for d in (0, -1, 1) for f in (low, high)], None))

    for d1 in DISTANCES:
        arrived(shard(d1, 2), R_SECOND + 3 * DISTANCES.index(d1) + 2)
        to_sibling(d1, 2)
    arrived(own_keys(core, 2), R_A + 2)
    pass_on(own_keys(core, 2), R_ASIB + 3, sibling)
    for d1 in DISTANCES:
        from_sibling(d1, 2)
    arrived(qp, R_QP)

    place_in_x = (2 * zh) * 128 + y * 32
    for t in (3, 2, 1, 0):
        rows = iota(1024, 0)
        mask = iota(1024, 1) <= place_in_x + ((rows // 32) % 2) * 128 + rows % 32
        _top, total, acc = attend(
            prompt_tile(t), [slab(i) for i in range(t)] + [slab(t, mask)], None)
        out = (acc / total).astype(jnp.bfloat16)
        for j in range(4):
            for c in range(4):
                r = j * 64 + c * 16
                op[4 * t + c, :, j * DH:(j + 1) * DH] = out[r:r + 16]
        for c in range(4):
            g = 4 * t + c
            dst = cut(po, me, QW)

            @pl.when(g != me)
            def _(g=g, c=c, dst=dst):
                remote(op.at[g], dst, pout_sems.at[g], R_OP,
                       place(t, zh * 2 + c // 2, y, c % 2)).start()

            @pl.when(g == me)
            def _(g=g, dst=dst):
                pltpu.make_async_copy(op.at[g], dst, recv_sems.at[R_OP]).start()

    for dy, r in ((0, 0), (-1, 1), (1, 2), (2, 3)):
        arrived(own_keys(other, dy), R_ASIB + r)

    @pl.loop(0, 8)
    def _(i):
        d = 7 - i
        t, xx, zz = chip_at(d // 2, d % 2)
        rows = iota(512, 0)
        mask = iota(512, 1) <= (t % 2) * 256 + y * 64 + rows % 64
        own_piece = (
            lambda: akv[0, xx].reshape(512, DH), lambda: akv[1, xx].reshape(512, DH), mask)
        _top, total, acc = attend(answer_tile(t), [low(2), high(2), own_piece], kept(t))
        out = (acc / total).astype(jnp.bfloat16)
        for j in range(4):
            for c in range(2):
                r = j * 64 + c * 32
                oa[2 * t + c, :, j * DH:(j + 1) * DH] = out[r:r + 32]
        dst = cut(ao, me, QW)
        remote(oa.at[2 * t + other], dst, aout_sems.at[i], R_OA, place(xx, zz, y, other)).start()

        @pl.when(i < 7)
        def _():
            remote(oa.at[2 * t + core], dst, aout_sems.at[8 + i], R_OA,
                   place(xx, zz, y, core)).start()

        @pl.when(i == 7)
        def _():
            pltpu.make_async_copy(oa.at[me], dst, recv_sems.at[R_OA]).start()

    assert len(sends) <= N_SEND
    for copy in sends:
        copy.wait_send()

    @pl.when(core != mine)
    def _():
        for copy in own_sends:
            copy.wait_send()

    for g in range(16):
        @pl.when(g != me)
        def _(g=g):
            pltpu.make_async_copy(op.at[g], op.at[g], pout_sems.at[g]).wait()

    for i in range(15):
        pltpu.make_async_copy(oa.at[i], oa.at[i], aout_sems.at[i]).wait()
    arrived(po, R_OP)
    arrived(ao, R_OA)


def shards(pq, pk, pv, aq, ak, av, answer_lengths):
    bf16, f32 = jnp.bfloat16, jnp.float32
    any_spec = pl.BlockSpec(memory_space=pl.ANY)
    prompt_out, answer_out = pl.pallas_call(
        kernel,
        out_shape=(
            jax.ShapeDtypeStruct(pq.shape, bf16),
            jax.ShapeDtypeStruct(aq.shape, bf16),
        ),
        in_specs=[any_spec] * 6,
        out_specs=(any_spec, any_spec),
        scratch_shapes=[
            pltpu.VMEM((2, 4, 4, 2, 4, 32, DH), bf16),
            pltpu.VMEM((2, 4, 2, 4, 64, DH), bf16),
            pltpu.VMEM((16, 16, QW), bf16),
            pltpu.VMEM((16, 32, QW), bf16),
            pltpu.VMEM((16, 16, QW), bf16),
            pltpu.VMEM((16, 32, QW), bf16),
            pltpu.VMEM((8, 256, DH), f32),
            pltpu.VMEM((8, 256, DH), f32),
            pltpu.VMEM((8, 256, DH), f32),
            pltpu.SemaphoreType.DMA((N_SEND,)),
            pltpu.SemaphoreType.DMA((16,)),
            pltpu.SemaphoreType.DMA((20,)),
            pltpu.SemaphoreType.DMA((N_RECV,)),
        ],
        compiler_params=pltpu.CompilerParams(
            collective_id=0, has_side_effects=True, vmem_limit_bytes=60 * 1024 * 1024),
        cost_estimate=pl.CostEstimate(
            flops=6_400_000_000, bytes_accessed=2_000_000, transcendentals=12_000_000),
    )(pq, pk, pv, aq, ak, av)
    seq, resp = lax.axis_index("seq"), lax.axis_index("resp")
    height = aq.shape[0]
    places = (seq % 2) * 256 + resp * height + jnp.arange(height, dtype=jnp.int32)
    live = lax.dynamic_index_in_dim(answer_lengths, seq // 2, 0, keepdims=False)
    answer_out = jnp.where((places < live)[:, None], answer_out, jnp.zeros((), bf16))
    return prompt_out, answer_out


def solution(mesh):
    rows = P(("prompt", "seq", "resp"), None)
    return jax.shard_map(
        shards,
        mesh=mesh,
        in_specs=(rows,) * 6 + (P("prompt"),),
        out_specs=(rows, rows),
        check_vma=False,
    )
```

```python
import math

import jax
import jax.numpy as jnp
from jax import lax
from jax.experimental import pallas as pl
from jax.experimental.pallas import tpu as pltpu
from jax.sharding import PartitionSpec as P

DH = 128
ZN = 8
QW = 4 * DH
SCALE = math.log2(math.e) / math.sqrt(DH)
BIG_NEG = -1e30
MESH = pl.DeviceIdType.MESH

R_KV, R_AKV, R_QP, R_QA, R_OP, R_OA, R_A = 0, 1, 2, 3, 4, 5, 6
R_FIRST, R_SECOND, R_SIB, R_ASIB = 9, 12, 24, 40
N_RECV = 44
N_SEND = 112
DISTANCES = (0, -1, 1, 2)


def dot_t(a, b):
    return lax.dot_general(a, b, (((1,), (1,)), ((), ())), preferred_element_type=jnp.float32)


def fold_max(s, top):
    for i in range(s.shape[1] // DH):
        c = s[:, i * DH:(i + 1) * DH]
        top = c if top is None else jnp.maximum(top, c)
    return top


def score_piece(item, i, top):
    keys, _values, mask = item.pieces[i]
    s = dot_t(item.q, keys())
    if mask is not None:
        s = jnp.where(mask(), s, BIG_NEG)
    item.buffer(i)[...] = s
    return fold_max(s, top)


def weigh_piece(item, i, top, acc):
    _keys, values, _mask = item.pieces[i]
    p = jnp.exp2((item.buffer(i)[...] - top) * SCALE).astype(jnp.bfloat16)
    v = values()
    v = jnp.concatenate([v, jnp.ones(v.shape, v.dtype)], axis=1)
    part = jnp.dot(p, v, preferred_element_type=jnp.float32)
    return part if acc is None else acc + part


def row_top(folded, old):
    top = jnp.max(folded, axis=1, keepdims=True)
    return top if old is None else jnp.maximum(top, old)


class Item:
    def __init__(self, load, pieces, buffer, state=None):
        self.load, self.pieces, self.buffer, self.state = load, pieces, buffer, state


def run_items(items, between):
    top = None
    for n in range(len(items) + 1):
        new = items[n] if n < len(items) else None
        now = items[n - 1] if n > 0 else None
        folded, acc = None, None
        if new is not None:
            new.q = new.load()
        for i in range(max(len(v.pieces) for v in (new, now) if v is not None)):
            if new is not None and i < len(new.pieces):
                folded = score_piece(new, i, folded)
            if now is not None and i < len(now.pieces):
                acc = weigh_piece(now, i, top, acc)
        if now is not None and now.state is not None:
            old_top, old_acc = now.state()
            acc = acc + old_acc * jnp.exp2((old_top - top) * SCALE)
        now_top = top
        if new is not None:
            top = row_top(folded, None if new.state is None else new.state()[0])
        if now is not None:
            between(n - 1, now_top, acc)


def kernel(pq, pk, pv, aq, ak, av, po, ao, kv, akv, qp, qa, op, oa, accs, tops, s0, s1,
           send_sems, pout_sems, aout_sems, recv_sems):
    part = lax.axis_index("prompt")
    seq = lax.axis_index("seq")
    resp = lax.axis_index("resp")
    x, z = seq // ZN, seq % ZN
    y, core = resp // 2, resp % 2
    zh, zb = z // 2, z % 2
    chip = x * 2 + zb
    me = chip * 2 + core
    mine, other = x // 2, 1 - core

    def place(xx, zz, yy, cc):
        return (part, xx * ZN + zz, yy * 2 + cc)

    def chip_at(dx, dz):
        x2, zb2 = (x + dx) % 4, (zb + dz) % 2
        return x2 * 2 + zb2, x2, zh * 2 + zb2

    def around(v, d):
        return (v + d + 4) % 4

    def first(d):
        return place(x, around(zh, (1 - core) * d) * 2 + zb, around(y, core * d), core)

    def second(d):
        return place(x, around(zh, core * d) * 2 + zb, around(y, (1 - core) * d), core)

    def y_dev(d):
        return place(x, z, around(y, d), core)

    sibling = place(x, z, y, other)
    chips = [chip_at(d // 2, d % 2) for d in range(8)]
    members = [
        (h * 2 + (core + dc) % 2, place(xx, zz, y, (core + dc) % 2))
        for h, xx, zz in chips for dc in range(2)
    ]
    partners = [dev for _, dev in members[1:]] + [first(1), first(-1), second(1), second(-1)]

    barrier = pltpu.get_barrier_semaphore()
    for dev in partners:
        pl.semaphore_signal(barrier, inc=1, device_id=dev, device_id_type=MESH)

    def cut(ref, h, width):
        return ref.at[:, pl.ds(pl.multiple_of(h * width, width), width)]

    rows_p = pl.ds(pl.multiple_of(core * 16, 16), 16)
    rows_a = pl.ds(pl.multiple_of(core * 32, 32), 32)
    k_land, v_land = kv.at[0, x, zh, zb, y, rows_p], kv.at[1, x, zh, zb, y, rows_p]
    ak_land, av_land = akv.at[0, x, zb, y, rows_a], akv.at[1, x, zb, y, rows_a]

    pltpu.make_async_copy(cut(pq, me, QW), qp.at[me], recv_sems.at[R_QP]).start()
    pltpu.make_async_copy(cut(aq, me, QW), qa.at[me], recv_sems.at[R_QA]).start()
    own_parts = (
        (cut(pk, chip, DH), k_land, R_KV), (cut(pv, chip, DH), v_land, R_KV),
        (cut(ak, chip, DH), ak_land, R_AKV), (cut(av, chip, DH), av_land, R_AKV))

    @pl.when(core == mine)
    def _():
        for src, dst, r in own_parts:
            pltpu.make_async_copy(src, dst, recv_sems.at[r]).start()

    pl.semaphore_wait(barrier, len(partners))

    sends = []

    def remote(src, dst, send_sem, r, dev):
        return pltpu.make_async_remote_copy(
            src_ref=src, dst_ref=dst, send_sem=send_sem,
            recv_sem=recv_sems.at[r], device_id=dev, device_id_type=MESH)

    def send(src, dst, r, dev):
        copy = remote(src, dst, send_sems.at[len(sends)], r, dev)
        copy.start()
        sends.append(copy)

    def pass_on(ref, r, dev):
        send(ref, ref, r, dev)

    def arrived(ref, r):
        pltpu.make_async_copy(ref, ref, recv_sems.at[r]).wait()

    own_sends = [remote(src, dst, aout_sems.at[16 + i], r, sibling)
                 for i, (src, dst, r) in enumerate(own_parts)]

    def part_of(c, d1, d2, n=slice(None)):
        zz = around(zh, (1 - c) * d1 + c * d2)
        yy = around(y, (1 - c) * d2 + c * d1)
        return kv.at[n, pl.ds(2 * c, 2), zz, :, yy]

    def shard(d1, d2):
        return part_of(core, d1, d2)

    def to_sibling(d1, d2):
        k = DISTANCES.index(d2) * 4 + DISTANCES.index(d1)
        pass_on(shard(d1, d2), R_SIB + k, sibling)

    def from_sibling(d1, d2):
        k = DISTANCES.index(d2) * 4 + DISTANCES.index(d1)
        arrived(part_of(other, d1, d2), R_SIB + k)

    def start_second(d1):
        r = R_SECOND + 3 * DISTANCES.index(d1)
        pass_on(shard(d1, 0), r, second(1))
        pass_on(shard(d1, 0), r + 1, second(-1))

    def middle_second(d1):
        r = R_SECOND + 3 * DISTANCES.index(d1)
        arrived(shard(d1, -1), r)
        pass_on(part_of(core, d1, -1, 0), r + 2, second(1))
        arrived(shard(d1, 1), r + 1)
        pass_on(part_of(core, d1, 1, 1), r + 2, second(-1))
        to_sibling(d1, -1)
        to_sibling(d1, 1)

    for d in (7, 6, 5, 4, 3, 2, 1):
        h, xx, zz = chips[d]
        send(cut(pk, h, DH), k_land, R_KV, place(xx, zz, y, mine))
        send(cut(pv, h, DH), v_land, R_KV, place(xx, zz, y, mine))

    @pl.when(core != mine)
    def _():
        for copy in own_sends:
            copy.start()

    arrived(shard(0, 0), R_KV)
    pass_on(shard(0, 0), R_FIRST, first(1))
    pass_on(shard(0, 0), R_FIRST + 1, first(-1))
    start_second(0)
    to_sibling(0, 0)
    for g, dev in members[:0:-1]:
        send(cut(aq, g, QW), qa.at[me], R_QA, dev)
    arrived(shard(-1, 0), R_FIRST)
    pass_on(part_of(core, -1, 0, 0), R_FIRST + 2, first(1))
    arrived(shard(1, 0), R_FIRST + 1)
    pass_on(part_of(core, 1, 0, 1), R_FIRST + 2, first(-1))
    start_second(-1)
    start_second(1)
    to_sibling(-1, 0)
    to_sibling(1, 0)
    for d in (7, 6, 5, 4, 3, 2, 1):
        h, xx, zz = chips[d]
        send(cut(ak, h, DH), ak_land, R_AKV, place(xx, zz, y, mine))
        send(cut(av, h, DH), av_land, R_AKV, place(xx, zz, y, mine))
    middle_second(0)
    arrived(shard(2, 0), R_FIRST + 2)
    start_second(2)
    to_sibling(2, 0)
    for g, dev in members[:0:-1]:
        send(cut(pq, g, QW), qp.at[me], R_QP, dev)

    def own_keys(c, dy, n=slice(None)):
        return akv.at[n, pl.ds(2 * c, 2), :, around(y, dy)]

    arrived(own_keys(core, 0), R_AKV)
    pass_on(own_keys(core, 0), R_A, y_dev(1))
    pass_on(own_keys(core, 0), R_A + 1, y_dev(-1))
    pass_on(own_keys(core, 0), R_ASIB, sibling)
    middle_second(-1)
    middle_second(1)
    middle_second(2)
    bufs = (s0, s1)

    def low(dy):
        def take(n):
            return kv[n, 0:2, :, :, around(y, dy)].reshape(512, DH)
        return (lambda: take(0), lambda: take(1), None)

    def high(dz):
        def take(n):
            return kv[n, 2:4, around(zh, dz)].reshape(512, DH)
        return (lambda: take(0), lambda: take(1), None)

    def half_slab(xx, h, mask=None):
        def take(n):
            return kv[n, xx, 2 * h:2 * h + 2].reshape(512, DH)
        return (lambda: take(0), lambda: take(1), mask)

    def iota(height, axis):
        return lax.broadcasted_iota(jnp.int32, (height, 512), axis)

    def answer_tile(t):
        return jnp.concatenate(
            [qa[4 * t + c, :, j * DH:(j + 1) * DH] for j in range(4) for c in range(4)], axis=0)

    def prompt_tile(t):
        return jnp.concatenate(
            [qp[4 * t + c, :, j * DH:(j + 1) * DH] for j in range(4) for c in range(4)], axis=0)

    def wide(b):
        return lambda i: bufs[b].at[i]

    def tall(b):
        return lambda i: bufs[b].at[i // 2, (i % 2) * 256:(i % 2) * 256 + 256]

    for d2 in (0, -1, 1):
        for d1 in DISTANCES:
            from_sibling(d1, d2)
    arrived(qa, R_QA)

    first_items = [
        Item(lambda t=t: answer_tile(t),
             [f(d) for d in (0, -1, 1) for f in (low, high)], wide(t % 2))
        for t in range(4)]

    def after_first(n, top, acc):
        tops[n] = jnp.broadcast_to(top, (512, DH))
        accs[n] = acc
        if n == 1:
            arrived(own_keys(core, -1), R_A)
            pass_on(own_keys(core, -1, 0), R_A + 2, y_dev(1))
            arrived(own_keys(core, 1), R_A + 1)
            pass_on(own_keys(core, 1, 1), R_A + 2, y_dev(-1))
            pass_on(own_keys(core, -1), R_ASIB + 1, sibling)
            pass_on(own_keys(core, 1), R_ASIB + 2, sibling)
        if n == 2:
            for d1 in DISTANCES:
                arrived(shard(d1, 2), R_SECOND + 3 * DISTANCES.index(d1) + 2)
                to_sibling(d1, 2)

    run_items(first_items, after_first)

    for d1 in DISTANCES:
        from_sibling(d1, 2)
    arrived(qp, R_QP)
    arrived(own_keys(core, 2), R_A + 2)
    pass_on(own_keys(core, 2), R_ASIB + 3, sibling)

    def prompt_mask(h):
        rows = iota(256, 0)
        here = (2 * zh) * 128 + y * 32 + ((rows // 32) % 2) * 128 + rows % 32
        return iota(256, 1) + h * 512 <= here

    def answer_mask():
        rows = iota(512, 0)
        return iota(512, 1) <= ((rows // 64) % 2) * 256 + y * 64 + rows % 64

    prompt_order = (3, 2, 1, 0)
    answer_order = (2, 1, 3, 0)
    second_items = []
    for t in prompt_order:
        pieces = [half_slab(i, h) for i in range(t) for h in range(2)]
        pieces += [half_slab(t, h, lambda h=h: prompt_mask(h)) for h in range(2)]
        second_items.append(Item(lambda t=t: prompt_tile(t), pieces, tall(len(second_items) % 2)))
    for dx in answer_order:
        t = (x + dx) % 4
        own_piece = (
            lambda t=t: akv[0, t].reshape(512, DH), lambda t=t: akv[1, t].reshape(512, DH),
            answer_mask)
        second_items.append(Item(
            lambda t=t: answer_tile(t), [low(2), high(2), own_piece], wide(len(second_items) % 2),
            lambda t=t: (tops[t][:, :1], accs[t])))

    def finished(acc):
        return (acc[:, :DH] / acc[:, DH:]).astype(jnp.bfloat16)

    def after_second(n, top, acc):
        if n < 4:
            t = prompt_order[n]
            out = finished(acc)
            for j in range(4):
                for c in range(4):
                    r = j * 64 + c * 16
                    op[4 * t + c, :, j * DH:(j + 1) * DH] = out[r:r + 16]
            for c in range(4):
                g = 4 * t + c
                dst = cut(po, me, QW)

                @pl.when(g != me)
                def _(g=g, c=c, dst=dst):
                    remote(op.at[g], dst, pout_sems.at[g], R_OP,
                           place(t, zh * 2 + c // 2, y, c % 2)).start()

                @pl.when(g == me)
                def _(g=g, dst=dst):
                    pltpu.make_async_copy(op.at[g], dst, recv_sems.at[R_OP]).start()
            if n == 2:
                for dy, r in ((0, 0), (-1, 1), (1, 2), (2, 3)):
                    arrived(own_keys(other, dy), R_ASIB + r)
            return
        dx = answer_order[n - 4]
        t = (x + dx) % 4
        out = finished(acc)
        for j in range(4):
            for c in range(4):
                r = j * 128 + c * 32
                oa[4 * t + c, :, j * DH:(j + 1) * DH] = out[r:r + 32]
        dst = cut(ao, me, QW)
        for k in (3, 2, 1, 0):
            d = dx * 4 + k
            g, dev = members[d]
            if d:
                remote(oa.at[g], dst, aout_sems.at[d], R_OA, dev).start()
            else:
                pltpu.make_async_copy(oa.at[g], dst, recv_sems.at[R_OA]).start()

    run_items(second_items, after_second)

    assert len(sends) <= N_SEND
    for copy in sends:
        copy.wait_send()

    @pl.when(core != mine)
    def _():
        for copy in own_sends:
            copy.wait_send()

    for g in range(16):
        @pl.when(g != me)
        def _(g=g):
            pltpu.make_async_copy(op.at[g], op.at[g], pout_sems.at[g]).wait()

    for i in range(1, 16):
        pltpu.make_async_copy(oa.at[i], oa.at[i], aout_sems.at[i]).wait()
    arrived(po, R_OP)
    arrived(ao, R_OA)


def shards(pq, pk, pv, aq, ak, av, answer_lengths):
    bf16, f32 = jnp.bfloat16, jnp.float32
    any_spec = pl.BlockSpec(memory_space=pl.ANY)
    prompt_out, answer_out = pl.pallas_call(
        kernel,
        out_shape=(
            jax.ShapeDtypeStruct(pq.shape, bf16),
            jax.ShapeDtypeStruct(aq.shape, bf16),
        ),
        in_specs=[any_spec] * 6,
        out_specs=(any_spec, any_spec),
        scratch_shapes=[
            pltpu.VMEM((2, 4, 4, 2, 4, 32, DH), bf16),
            pltpu.VMEM((2, 4, 2, 4, 64, DH), bf16),
            pltpu.VMEM((16, 16, QW), bf16),
            pltpu.VMEM((16, 32, QW), bf16),
            pltpu.VMEM((16, 16, QW), bf16),
            pltpu.VMEM((16, 32, QW), bf16),
            pltpu.VMEM((4, 512, 2 * DH), f32),
            pltpu.VMEM((4, 512, DH), f32),
            pltpu.VMEM((6, 512, 512), f32),
            pltpu.VMEM((6, 512, 512), f32),
            pltpu.SemaphoreType.DMA((N_SEND,)),
            pltpu.SemaphoreType.DMA((16,)),
            pltpu.SemaphoreType.DMA((20,)),
            pltpu.SemaphoreType.DMA((N_RECV,)),
        ],
        compiler_params=pltpu.CompilerParams(
            collective_id=0, has_side_effects=True, vmem_limit_bytes=60 * 1024 * 1024),
        cost_estimate=pl.CostEstimate(
            flops=6_400_000_000, bytes_accessed=2_000_000, transcendentals=12_000_000),
    )(pq, pk, pv, aq, ak, av)
    seq, resp = lax.axis_index("seq"), lax.axis_index("resp")
    height = aq.shape[0]
    places = (seq % 2) * 256 + resp * height + jnp.arange(height, dtype=jnp.int32)
    live = lax.dynamic_index_in_dim(answer_lengths, seq // 2, 0, keepdims=False)
    answer_out = jnp.where((places < live)[:, None], answer_out, jnp.zeros((), bf16))
    return prompt_out, answer_out


def solution(mesh):
    rows = P(("prompt", "seq", "resp"), None)
    return jax.shard_map(
        shards,
        mesh=mesh,
        in_specs=(rows,) * 6 + (P("prompt"),),
        out_specs=(rows, rows),
        check_vma=False,
    )
```

```python
import math

import jax
import jax.numpy as jnp
from jax import lax
from jax.experimental import pallas as pl
from jax.experimental.pallas import tpu as pltpu
from jax.sharding import PartitionSpec as P

DH = 128
ZN = 8
QW = 4 * DH
SCALE = math.log2(math.e) / math.sqrt(DH)
BIG_NEG = -1e30
MESH = pl.DeviceIdType.MESH

R_KV, R_AKV, R_QP, R_QA, R_OP, R_OA, R_A = 0, 1, 2, 3, 4, 5, 6
R_FIRST, R_SECOND, R_SIB, R_ASIB = 9, 12, 24, 40
N_RECV = 44
N_SEND = 112
DISTANCES = (0, -1, 1, 2)


def dot_t(a, b):
    return lax.dot_general(a, b, (((1,), (1,)), ((), ())), preferred_element_type=jnp.float32)


def fold_max(s, top):
    for i in range(s.shape[1] // DH):
        c = s[:, i * DH:(i + 1) * DH]
        top = c if top is None else jnp.maximum(top, c)
    return top


def score_piece(item, i, top):
    keys, _values, mask = item.pieces[i]
    s = dot_t(item.q, keys())
    if mask is not None:
        s = jnp.where(mask(), s, BIG_NEG)
    item.buffer(i)[...] = s
    return fold_max(s, top)


def weigh_piece(item, i, top, acc):
    _keys, values, _mask = item.pieces[i]
    p = jnp.exp2((item.buffer(i)[...] - top) * SCALE).astype(jnp.bfloat16)
    v = values()
    v = jnp.concatenate([v, jnp.ones(v.shape, v.dtype)], axis=1)
    part = jnp.dot(p, v, preferred_element_type=jnp.float32)
    return part if acc is None else acc + part


def row_top(folded, old):
    top = jnp.max(folded, axis=1, keepdims=True)
    return top if old is None else jnp.maximum(top, old)


class Item:
    def __init__(self, load, pieces, buffer, state=None):
        self.load, self.pieces, self.buffer, self.state = load, pieces, buffer, state


def run_items(items, between):
    top = None
    for n in range(len(items) + 1):
        new = items[n] if n < len(items) else None
        now = items[n - 1] if n > 0 else None
        folded, acc = None, None
        if new is not None:
            new.q = new.load()
        for i in range(max(len(v.pieces) for v in (new, now) if v is not None)):
            if new is not None and i < len(new.pieces):
                folded = score_piece(new, i, folded)
            if now is not None and i < len(now.pieces):
                acc = weigh_piece(now, i, top, acc)
        if now is not None and now.state is not None:
            old_top, old_acc = now.state()
            acc = acc + old_acc * jnp.exp2((old_top - top) * SCALE)
        now_top = top
        if new is not None:
            top = row_top(folded, None if new.state is None else new.state()[0])
        if now is not None:
            between(n - 1, now_top, acc)


def kernel(pq, pk, pv, aq, ak, av, po, ao, kv, akv, qp, qa, op, oa, accs, tops, s0, s1,
           send_sems, pout_sems, aout_sems, recv_sems):
    part = lax.axis_index("prompt")
    seq = lax.axis_index("seq")
    resp = lax.axis_index("resp")
    x, z = seq // ZN, seq % ZN
    y, core = resp // 2, resp % 2
    zh, zb = z // 2, z % 2
    chip = x * 2 + zb
    me = chip * 2 + core
    mine, other = x // 2, 1 - core

    def place(xx, zz, yy, cc):
        return (part, xx * ZN + zz, yy * 2 + cc)

    def chip_at(dx, dz):
        x2, zb2 = (x + dx) % 4, (zb + dz) % 2
        return x2 * 2 + zb2, x2, zh * 2 + zb2

    def around(v, d):
        return (v + d + 4) % 4

    def first(d):
        return place(x, around(zh, (1 - core) * d) * 2 + zb, around(y, core * d), core)

    def second(d):
        return place(x, around(zh, core * d) * 2 + zb, around(y, (1 - core) * d), core)

    def y_dev(d):
        return place(x, z, around(y, d), core)

    sibling = place(x, z, y, other)
    chips = [chip_at(d // 2, d % 2) for d in range(8)]
    members = [
        (h * 2 + (core + dc) % 2, place(xx, zz, y, (core + dc) % 2))
        for h, xx, zz in chips for dc in range(2)
    ]
    partners = [dev for _, dev in members[1:]] + [f(d) for f in (first, second) for d in (1, -1, 2)]

    barrier = pltpu.get_barrier_semaphore()
    for dev in partners:
        pl.semaphore_signal(barrier, inc=1, device_id=dev, device_id_type=MESH)

    def cut(ref, h, width):
        return ref.at[:, pl.ds(pl.multiple_of(h * width, width), width)]

    rows_p = pl.ds(pl.multiple_of(core * 16, 16), 16)
    rows_a = pl.ds(pl.multiple_of(core * 32, 32), 32)
    k_land, v_land = kv.at[0, x, zh, zb, y, rows_p], kv.at[1, x, zh, zb, y, rows_p]
    ak_land, av_land = akv.at[0, x, zb, y, rows_a], akv.at[1, x, zb, y, rows_a]

    pltpu.make_async_copy(cut(pq, me, QW), qp.at[me], recv_sems.at[R_QP]).start()
    pltpu.make_async_copy(cut(aq, me, QW), qa.at[me], recv_sems.at[R_QA]).start()
    own_parts = (
        (cut(pk, chip, DH), k_land, R_KV), (cut(pv, chip, DH), v_land, R_KV),
        (cut(ak, chip, DH), ak_land, R_AKV), (cut(av, chip, DH), av_land, R_AKV))

    @pl.when(core == mine)
    def _():
        for src, dst, r in own_parts:
            pltpu.make_async_copy(src, dst, recv_sems.at[r]).start()

    pl.semaphore_wait(barrier, len(partners))

    sends = []

    def remote(src, dst, send_sem, r, dev):
        return pltpu.make_async_remote_copy(
            src_ref=src, dst_ref=dst, send_sem=send_sem,
            recv_sem=recv_sems.at[r], device_id=dev, device_id_type=MESH)

    def send(src, dst, r, dev):
        copy = remote(src, dst, send_sems.at[len(sends)], r, dev)
        copy.start()
        sends.append(copy)

    def pass_on(ref, r, dev):
        send(ref, ref, r, dev)

    def arrived(ref, r):
        pltpu.make_async_copy(ref, ref, recv_sems.at[r]).wait()

    own_sends = [remote(src, dst, aout_sems.at[16 + i], r, sibling)
                 for i, (src, dst, r) in enumerate(own_parts)]

    def part_of(c, d1, d2, n=slice(None)):
        zz = around(zh, (1 - c) * d1 + c * d2)
        yy = around(y, (1 - c) * d2 + c * d1)
        return kv.at[n, pl.ds(2 * c, 2), zz, :, yy]

    def shard(d1, d2):
        return part_of(core, d1, d2)

    def to_sibling(d1, d2):
        k = DISTANCES.index(d2) * 4 + DISTANCES.index(d1)
        pass_on(shard(d1, d2), R_SIB + k, sibling)

    def from_sibling(d1, d2):
        k = DISTANCES.index(d2) * 4 + DISTANCES.index(d1)
        arrived(part_of(other, d1, d2), R_SIB + k)

    def start_first():
        for k, d in enumerate((1, -1, 2)):
            pass_on(shard(0, 0), R_FIRST + k, first(d))

    def start_second(d1):
        r = R_SECOND + 3 * DISTANCES.index(d1)
        for k, d in enumerate((1, -1, 2)):
            pass_on(shard(d1, 0), r + k, second(d))

    def hand_over(d1, d2):
        k = DISTANCES[1:].index(d2)
        arrived(shard(d1, d2), R_SECOND + 3 * DISTANCES.index(d1) + k)
        to_sibling(d1, d2)

    for d in (7, 6, 5, 4, 3, 2, 1):
        h, xx, zz = chips[d]
        send(cut(pk, h, DH), k_land, R_KV, place(xx, zz, y, mine))
        send(cut(pv, h, DH), v_land, R_KV, place(xx, zz, y, mine))

    @pl.when(core != mine)
    def _():
        for copy in own_sends:
            copy.start()

    arrived(shard(0, 0), R_KV)
    start_first()
    start_second(0)
    to_sibling(0, 0)
    for g, dev in members[:0:-1]:
        send(cut(aq, g, QW), qa.at[me], R_QA, dev)
    for k, d1 in enumerate((-1, 1, 2)):
        arrived(shard(d1, 0), R_FIRST + k)
        start_second(d1)
        to_sibling(d1, 0)
    for d in (7, 6, 5, 4, 3, 2, 1):
        h, xx, zz = chips[d]
        send(cut(ak, h, DH), ak_land, R_AKV, place(xx, zz, y, mine))
        send(cut(av, h, DH), av_land, R_AKV, place(xx, zz, y, mine))
    for g, dev in members[:0:-1]:
        send(cut(pq, g, QW), qp.at[me], R_QP, dev)

    def own_keys(c, dy, n=slice(None)):
        return akv.at[n, pl.ds(2 * c, 2), :, around(y, dy)]

    bufs = (s0, s1)

    def low(dy):
        def take(n):
            return kv[n, 0:2, :, :, around(y, dy)].reshape(512, DH)
        return (lambda: take(0), lambda: take(1), None)

    def high(dz):
        def take(n):
            return kv[n, 2:4, around(zh, dz)].reshape(512, DH)
        return (lambda: take(0), lambda: take(1), None)

    def half_slab(xx, h, mask=None):
        def take(n):
            return kv[n, xx, 2 * h:2 * h + 2].reshape(512, DH)
        return (lambda: take(0), lambda: take(1), mask)

    def iota(height, axis):
        return lax.broadcasted_iota(jnp.int32, (height, 512), axis)

    def answer_tile(t):
        return jnp.concatenate(
            [qa[4 * t + c, :, j * DH:(j + 1) * DH] for j in range(4) for c in range(4)], axis=0)

    def prompt_tile(t):
        return jnp.concatenate(
            [qp[4 * t + c, :, j * DH:(j + 1) * DH] for j in range(4) for c in range(4)], axis=0)

    def wide(b):
        return lambda i: bufs[b].at[i]

    def tall(b):
        return lambda i: bufs[b].at[i // 2, (i % 2) * 256:(i % 2) * 256 + 256]

    def keep(n, top, acc):
        tops[n] = jnp.broadcast_to(top, (512, DH))
        accs[n] = acc

    def kept(t):
        return tops[t][:, :1], accs[t]

    for d1 in DISTANCES:
        from_sibling(d1, 0)
    arrived(qa, R_QA)

    def after_first(n, top, acc):
        keep(n, top, acc)
        if n == 0:
            arrived(own_keys(core, 0), R_AKV)
            pass_on(own_keys(core, 0), R_A, y_dev(1))
            pass_on(own_keys(core, 0), R_A + 1, y_dev(-1))
            pass_on(own_keys(core, 0), R_ASIB, sibling)
        else:
            for d1 in ((), (0,), (-1, 1), (2,))[n]:
                hand_over(d1, -1)
                hand_over(d1, 1)

    run_items([
        Item(lambda t=t: answer_tile(t), [low(0), high(0)], wide(t % 2)) for t in range(4)
    ], after_first)

    for d1 in DISTANCES:
        from_sibling(d1, -1)
        from_sibling(d1, 1)

    def after_second(n, top, acc):
        keep(n, top, acc)
        if n == 1:
            arrived(own_keys(core, -1), R_A)
            pass_on(own_keys(core, -1, 0), R_A + 2, y_dev(1))
            arrived(own_keys(core, 1), R_A + 1)
            pass_on(own_keys(core, 1, 1), R_A + 2, y_dev(-1))
            pass_on(own_keys(core, -1), R_ASIB + 1, sibling)
            pass_on(own_keys(core, 1), R_ASIB + 2, sibling)
        for d1 in ((), (), (0, -1), (1, 2))[n]:
            hand_over(d1, 2)

    run_items([
        Item(lambda t=t: answer_tile(t), [f(d) for d in (-1, 1) for f in (low, high)],
             wide(t % 2), lambda t=t: kept(t))
        for t in range(4)
    ], after_second)

    for d1 in DISTANCES:
        from_sibling(d1, 2)
    arrived(qp, R_QP)

    def prompt_mask(h):
        rows = iota(256, 0)
        here = (2 * zh) * 128 + y * 32 + ((rows // 32) % 2) * 128 + rows % 32
        return iota(256, 1) + h * 512 <= here

    def answer_mask():
        rows = iota(512, 0)
        return iota(512, 1) <= ((rows // 64) % 2) * 256 + y * 64 + rows % 64

    prompt_order = (3, 2, 1, 0)
    answer_order = (2, 1, 3, 0)
    last_items = []
    for t in prompt_order:
        pieces = [half_slab(i, h) for i in range(t) for h in range(2)]
        pieces += [half_slab(t, h, lambda h=h: prompt_mask(h)) for h in range(2)]
        last_items.append(Item(lambda t=t: prompt_tile(t), pieces, tall(len(last_items) % 2)))
    for dx in answer_order:
        t = (x + dx) % 4
        own_piece = (
            lambda t=t: akv[0, t].reshape(512, DH), lambda t=t: akv[1, t].reshape(512, DH),
            answer_mask)
        last_items.append(Item(
            lambda t=t: answer_tile(t), [low(2), high(2), own_piece], wide(len(last_items) % 2),
            lambda t=t: kept(t)))

    def finished(acc):
        return (acc[:, :DH] / acc[:, DH:]).astype(jnp.bfloat16)

    def after_last(n, top, acc):
        if n < 4:
            t = prompt_order[n]
            out = finished(acc)
            for j in range(4):
                for c in range(4):
                    r = j * 64 + c * 16
                    op[4 * t + c, :, j * DH:(j + 1) * DH] = out[r:r + 16]
            for c in range(4):
                g = 4 * t + c
                dst = cut(po, me, QW)

                @pl.when(g != me)
                def _(g=g, c=c, dst=dst):
                    remote(op.at[g], dst, pout_sems.at[g], R_OP,
                           place(t, zh * 2 + c // 2, y, c % 2)).start()

                @pl.when(g == me)
                def _(g=g, dst=dst):
                    pltpu.make_async_copy(op.at[g], dst, recv_sems.at[R_OP]).start()
            if n == 1:
                arrived(own_keys(core, 2), R_A + 2)
                pass_on(own_keys(core, 2), R_ASIB + 3, sibling)
            if n == 2:
                for dy, r in ((0, 0), (-1, 1), (1, 2), (2, 3)):
                    arrived(own_keys(other, dy), R_ASIB + r)
            return
        dx = answer_order[n - 4]
        t = (x + dx) % 4
        out = finished(acc)
        for j in range(4):
            for c in range(4):
                r = j * 128 + c * 32
                oa[4 * t + c, :, j * DH:(j + 1) * DH] = out[r:r + 32]
        dst = cut(ao, me, QW)
        for k in (3, 2, 1, 0):
            d = dx * 4 + k
            g, dev = members[d]
            if d:
                remote(oa.at[g], dst, aout_sems.at[d], R_OA, dev).start()
            else:
                pltpu.make_async_copy(oa.at[g], dst, recv_sems.at[R_OA]).start()

    run_items(last_items, after_last)

    assert len(sends) <= N_SEND
    for copy in sends:
        copy.wait_send()

    @pl.when(core != mine)
    def _():
        for copy in own_sends:
            copy.wait_send()

    for g in range(16):
        @pl.when(g != me)
        def _(g=g):
            pltpu.make_async_copy(op.at[g], op.at[g], pout_sems.at[g]).wait()

    for i in range(1, 16):
        pltpu.make_async_copy(oa.at[i], oa.at[i], aout_sems.at[i]).wait()
    arrived(po, R_OP)
    arrived(ao, R_OA)


def closing(lengths, prompt_in, answer_in, prompt_out, answer_out):
    seq, resp = lax.axis_index("seq"), lax.axis_index("resp")
    height = answer_in.shape[0]
    live = lengths[seq // 2] - (seq % 2) * 256 - resp * height
    prompt_out[...] = prompt_in[...]
    for i in range(0, answer_in.shape[1], 1024):
        rows = lax.broadcasted_iota(jnp.int32, (height, 1024), 0)
        values = answer_in[:, i:i + 1024].astype(jnp.float32)
        answer_out[:, i:i + 1024] = jnp.where(rows < live, values, 0.0).astype(jnp.bfloat16)


def shards(pq, pk, pv, aq, ak, av, answer_lengths):
    bf16, f32 = jnp.bfloat16, jnp.float32
    any_spec = pl.BlockSpec(memory_space=pl.ANY)
    prompt_out, answer_out = pl.pallas_call(
        kernel,
        out_shape=(
            jax.ShapeDtypeStruct(pq.shape, bf16),
            jax.ShapeDtypeStruct(aq.shape, bf16),
        ),
        in_specs=[any_spec] * 6,
        out_specs=(any_spec, any_spec),
        scratch_shapes=[
            pltpu.VMEM((2, 4, 4, 2, 4, 32, DH), bf16),
            pltpu.VMEM((2, 4, 2, 4, 64, DH), bf16),
            pltpu.VMEM((16, 16, QW), bf16),
            pltpu.VMEM((16, 32, QW), bf16),
            pltpu.VMEM((16, 16, QW), bf16),
            pltpu.VMEM((16, 32, QW), bf16),
            pltpu.VMEM((4, 512, 2 * DH), f32),
            pltpu.VMEM((4, 512, DH), f32),
            pltpu.VMEM((6, 512, 512), f32),
            pltpu.VMEM((6, 512, 512), f32),
            pltpu.SemaphoreType.DMA((N_SEND,)),
            pltpu.SemaphoreType.DMA((16,)),
            pltpu.SemaphoreType.DMA((20,)),
            pltpu.SemaphoreType.DMA((N_RECV,)),
        ],
        compiler_params=pltpu.CompilerParams(
            collective_id=0, has_side_effects=True, vmem_limit_bytes=60 * 1024 * 1024),
        cost_estimate=pl.CostEstimate(
            flops=6_400_000_000, bytes_accessed=2_000_000, transcendentals=12_000_000),
    )(pq, pk, pv, aq, ak, av)
    vmem = pl.BlockSpec(memory_space=pltpu.VMEM)
    return pl.pallas_call(
        closing,
        out_shape=(
            jax.ShapeDtypeStruct(pq.shape, bf16),
            jax.ShapeDtypeStruct(aq.shape, bf16),
        ),
        in_specs=[pl.BlockSpec(memory_space=pltpu.SMEM), vmem, vmem],
        out_specs=(vmem, vmem),
        name="closing",
    )(answer_lengths, prompt_out, answer_out)


def solution(mesh):
    rows = P(("prompt", "seq", "resp"), None)
    return jax.shard_map(
        shards,
        mesh=mesh,
        in_specs=(rows,) * 6 + (P("prompt"),),
        out_specs=(rows, rows),
        check_vma=False,
    )
```

```python
import math

import jax
import jax.numpy as jnp
from jax import lax
from jax.experimental import pallas as pl
from jax.experimental.pallas import tpu as pltpu
from jax.sharding import PartitionSpec as P

DH = 128
ZN = 8
QW = 4 * DH
SCALE = math.log2(math.e) / math.sqrt(DH)
BIG_NEG = -1e30
MESH = pl.DeviceIdType.MESH

R_KV, R_AKV, R_QP, R_QA, R_OP, R_OA, R_A = 0, 1, 2, 3, 4, 5, 6
R_FIRST, R_SECOND, R_SIB, R_ASIB = 9, 12, 24, 40
N_RECV = 44
N_SEND = 112
DISTANCES = (0, -1, 1, 2)


def dot_t(a, b):
    return lax.dot_general(a, b, (((1,), (1,)), ((), ())), preferred_element_type=jnp.float32)


def fold_max(s, top):
    for i in range(s.shape[1] // DH):
        c = s[:, i * DH:(i + 1) * DH]
        top = c if top is None else jnp.maximum(top, c)
    return top


def score_piece(item, i, top):
    keys, _values, mask = item.pieces[i]
    s = dot_t(item.q, keys())
    if mask is not None:
        s = jnp.where(mask(), s, BIG_NEG)
    item.buffer(i)[...] = s
    return fold_max(s, top)


def weigh_piece(item, i, top, acc):
    _keys, values, _mask = item.pieces[i]
    p = jnp.exp2((item.buffer(i)[...] - top) * SCALE).astype(jnp.bfloat16)
    v = values()
    v = jnp.concatenate([v, jnp.ones(v.shape, v.dtype)], axis=1)
    part = jnp.dot(p, v, preferred_element_type=jnp.float32)
    return part if acc is None else acc + part


def row_top(folded, old):
    top = jnp.max(folded, axis=1, keepdims=True)
    return top if old is None else jnp.maximum(top, old)


class Item:
    def __init__(self, load, pieces, buffer, state=None):
        self.load, self.pieces, self.buffer, self.state = load, pieces, buffer, state


def run_items(items, between):
    top = None
    for n in range(len(items) + 1):
        new = items[n] if n < len(items) else None
        now = items[n - 1] if n > 0 else None
        folded, acc = None, None
        if new is not None:
            new.q = new.load()
        for i in range(max(len(v.pieces) for v in (new, now) if v is not None)):
            if new is not None and i < len(new.pieces):
                folded = score_piece(new, i, folded)
            if now is not None and i < len(now.pieces):
                acc = weigh_piece(now, i, top, acc)
        if now is not None and now.state is not None:
            old_top, old_acc = now.state()
            acc = acc + old_acc * jnp.exp2((old_top - top) * SCALE)
        now_top = top
        if new is not None:
            top = row_top(folded, None if new.state is None else new.state()[0])
        if now is not None:
            between(n - 1, now_top, acc)


def kernel(pq, pk, pv, aq, ak, av, po, ao, kv, akv, qp, qa, op, oa, accs, tops, s0, s1,
           send_sems, pout_sems, aout_sems, recv_sems):
    part = lax.axis_index("prompt")
    seq = lax.axis_index("seq")
    resp = lax.axis_index("resp")
    x, z = seq // ZN, seq % ZN
    y, core = resp // 2, resp % 2
    zh, zb = z // 2, z % 2
    chip = x * 2 + zb
    me = chip * 2 + core
    mine, other = x // 2, 1 - core

    def place(xx, zz, yy, cc):
        return (part, xx * ZN + zz, yy * 2 + cc)

    def chip_at(dx, dz):
        x2, zb2 = (x + dx) % 4, (zb + dz) % 2
        return x2 * 2 + zb2, x2, zh * 2 + zb2

    def around(v, d):
        return (v + d + 4) % 4

    def first(d):
        return place(x, around(zh, (1 - core) * d) * 2 + zb, around(y, core * d), core)

    def second(d):
        return place(x, around(zh, core * d) * 2 + zb, around(y, (1 - core) * d), core)

    def y_dev(d):
        return place(x, z, around(y, d), core)

    sibling = place(x, z, y, other)
    chips = [chip_at(d // 2, d % 2) for d in range(8)]
    members = [
        (h * 2 + (core + dc) % 2, place(xx, zz, y, (core + dc) % 2))
        for h, xx, zz in chips for dc in range(2)
    ]
    partners = [dev for _, dev in members[1:]] + [first(1), first(-1), first(2), second(1), second(-1)]

    barrier = pltpu.get_barrier_semaphore()
    for dev in partners:
        pl.semaphore_signal(barrier, inc=1, device_id=dev, device_id_type=MESH)

    def cut(ref, h, width):
        return ref.at[:, pl.ds(pl.multiple_of(h * width, width), width)]

    rows_p = pl.ds(pl.multiple_of(core * 16, 16), 16)
    rows_a = pl.ds(pl.multiple_of(core * 32, 32), 32)
    k_land, v_land = kv.at[0, x, zh, zb, y, rows_p], kv.at[1, x, zh, zb, y, rows_p]
    ak_land, av_land = akv.at[0, x, zb, y, rows_a], akv.at[1, x, zb, y, rows_a]

    pltpu.make_async_copy(cut(pq, me, QW), qp.at[me], recv_sems.at[R_QP]).start()
    pltpu.make_async_copy(cut(aq, me, QW), qa.at[me], recv_sems.at[R_QA]).start()
    own_parts = (
        (cut(pk, chip, DH), k_land, R_KV), (cut(pv, chip, DH), v_land, R_KV),
        (cut(ak, chip, DH), ak_land, R_AKV), (cut(av, chip, DH), av_land, R_AKV))

    @pl.when(core == mine)
    def _():
        for src, dst, r in own_parts:
            pltpu.make_async_copy(src, dst, recv_sems.at[r]).start()

    pl.semaphore_wait(barrier, len(partners))

    sends = []

    def remote(src, dst, send_sem, r, dev):
        return pltpu.make_async_remote_copy(
            src_ref=src, dst_ref=dst, send_sem=send_sem,
            recv_sem=recv_sems.at[r], device_id=dev, device_id_type=MESH)

    def send(src, dst, r, dev):
        copy = remote(src, dst, send_sems.at[len(sends)], r, dev)
        copy.start()
        sends.append(copy)

    def pass_on(ref, r, dev):
        send(ref, ref, r, dev)

    def arrived(ref, r):
        pltpu.make_async_copy(ref, ref, recv_sems.at[r]).wait()

    own_sends = [remote(src, dst, aout_sems.at[16 + i], r, sibling)
                 for i, (src, dst, r) in enumerate(own_parts)]

    def part_of(c, d1, d2, n=slice(None)):
        zz = around(zh, (1 - c) * d1 + c * d2)
        yy = around(y, (1 - c) * d2 + c * d1)
        return kv.at[n, pl.ds(2 * c, 2), zz, :, yy]

    def shard(d1, d2):
        return part_of(core, d1, d2)

    def to_sibling(d1, d2):
        k = DISTANCES.index(d2) * 4 + DISTANCES.index(d1)
        pass_on(shard(d1, d2), R_SIB + k, sibling)

    def from_sibling(d1, d2):
        k = DISTANCES.index(d2) * 4 + DISTANCES.index(d1)
        arrived(part_of(other, d1, d2), R_SIB + k)

    def start_first():
        for k, d in enumerate((1, -1, 2)):
            pass_on(shard(0, 0), R_FIRST + k, first(d))

    def start_second(d1):
        r = R_SECOND + 3 * DISTANCES.index(d1)
        pass_on(shard(d1, 0), r, second(1))
        pass_on(shard(d1, 0), r + 1, second(-1))

    def middle_second(d1):
        r = R_SECOND + 3 * DISTANCES.index(d1)
        arrived(shard(d1, -1), r)
        pass_on(part_of(core, d1, -1, 0), r + 2, second(1))
        arrived(shard(d1, 1), r + 1)
        pass_on(part_of(core, d1, 1, 1), r + 2, second(-1))
        to_sibling(d1, -1)
        to_sibling(d1, 1)

    def hand_over(d1):
        arrived(shard(d1, 2), R_SECOND + 3 * DISTANCES.index(d1) + 2)
        to_sibling(d1, 2)

    def own_keys(c, dy, n=slice(None)):
        return akv.at[n, pl.ds(2 * c, 2), :, around(y, dy)]

    for d in (7, 6, 5, 4, 3, 2, 1):
        h, xx, zz = chips[d]
        send(cut(pk, h, DH), k_land, R_KV, place(xx, zz, y, mine))
        send(cut(pv, h, DH), v_land, R_KV, place(xx, zz, y, mine))

    @pl.when(core != mine)
    def _():
        for copy in own_sends:
            copy.start()

    arrived(shard(0, 0), R_KV)
    start_first()
    start_second(0)
    to_sibling(0, 0)
    for g, dev in members[:0:-1]:
        send(cut(aq, g, QW), qa.at[me], R_QA, dev)
    for k, d1 in enumerate((-1, 1, 2)):
        arrived(shard(d1, 0), R_FIRST + k)
        start_second(d1)
        to_sibling(d1, 0)
    for d in (7, 6, 5, 4, 3, 2, 1):
        h, xx, zz = chips[d]
        send(cut(ak, h, DH), ak_land, R_AKV, place(xx, zz, y, mine))
        send(cut(av, h, DH), av_land, R_AKV, place(xx, zz, y, mine))
    for d1 in DISTANCES:
        middle_second(d1)
    arrived(own_keys(core, 0), R_AKV)
    pass_on(own_keys(core, 0), R_A, y_dev(1))
    pass_on(own_keys(core, 0), R_A + 1, y_dev(-1))
    pass_on(own_keys(core, 0), R_ASIB, sibling)
    for g, dev in members[:0:-1]:
        send(cut(pq, g, QW), qp.at[me], R_QP, dev)

    bufs = (s0, s1)

    def low(dy):
        def take(n):
            return kv[n, 0:2, :, :, around(y, dy)].reshape(512, DH)
        return (lambda: take(0), lambda: take(1), None)

    def high(dz):
        def take(n):
            return kv[n, 2:4, around(zh, dz)].reshape(512, DH)
        return (lambda: take(0), lambda: take(1), None)

    def half_slab(xx, h, mask=None):
        def take(n):
            return kv[n, xx, 2 * h:2 * h + 2].reshape(512, DH)
        return (lambda: take(0), lambda: take(1), mask)

    def iota(height, axis):
        return lax.broadcasted_iota(jnp.int32, (height, 512), axis)

    def answer_tile(t):
        return jnp.concatenate(
            [qa[4 * t + c, :, j * DH:(j + 1) * DH] for j in range(4) for c in range(4)], axis=0)

    def prompt_tile(t):
        return jnp.concatenate(
            [qp[4 * t + c, :, j * DH:(j + 1) * DH] for j in range(4) for c in range(4)], axis=0)

    def wide(b):
        return lambda i: bufs[b].at[i]

    def tall(b):
        return lambda i: bufs[b].at[i // 2, (i % 2) * 256:(i % 2) * 256 + 256]

    def keep(n, top, acc):
        tops[n] = jnp.broadcast_to(top, (512, DH))
        accs[n] = acc

    def kept(t):
        return tops[t][:, :1], accs[t]

    for d2 in (0, -1, 1):
        for d1 in DISTANCES:
            from_sibling(d1, d2)
    arrived(qa, R_QA)

    def after_first(n, top, acc):
        keep(n, top, acc)
        if n == 1:
            for d1 in DISTANCES:
                hand_over(d1)
        if n == 2:
            arrived(own_keys(core, -1), R_A)
            pass_on(own_keys(core, -1, 0), R_A + 2, y_dev(1))
            arrived(own_keys(core, 1), R_A + 1)
            pass_on(own_keys(core, 1, 1), R_A + 2, y_dev(-1))
            pass_on(own_keys(core, -1), R_ASIB + 1, sibling)
            pass_on(own_keys(core, 1), R_ASIB + 2, sibling)

    run_items([
        Item(lambda t=t: answer_tile(t),
             [f(d) for d in (0, -1, 1) for f in (low, high)], wide(t % 2))
        for t in range(4)
    ], after_first)

    for d1 in DISTANCES:
        from_sibling(d1, 2)
    arrived(qp, R_QP)

    def prompt_mask(h):
        rows = iota(256, 0)
        here = (2 * zh) * 128 + y * 32 + ((rows // 32) % 2) * 128 + rows % 32
        return iota(256, 1) + h * 512 <= here

    def answer_mask():
        rows = iota(512, 0)
        return iota(512, 1) <= ((rows // 64) % 2) * 256 + y * 64 + rows % 64

    prompt_order = (3, 2, 1, 0)
    answer_order = (2, 1, 3, 0)
    last_items = []
    for t in prompt_order:
        pieces = [half_slab(i, h) for i in range(t) for h in range(2)]
        pieces += [half_slab(t, h, lambda h=h: prompt_mask(h)) for h in range(2)]
        last_items.append(Item(lambda t=t: prompt_tile(t), pieces, tall(len(last_items) % 2)))
    for dx in answer_order:
        t = (x + dx) % 4
        own_piece = (
            lambda t=t: akv[0, t].reshape(512, DH), lambda t=t: akv[1, t].reshape(512, DH),
            answer_mask)
        last_items.append(Item(
            lambda t=t: answer_tile(t), [low(2), high(2), own_piece], wide(len(last_items) % 2),
            lambda t=t: kept(t)))

    def finished(acc):
        return (acc[:, :DH] / acc[:, DH:]).astype(jnp.bfloat16)

    def after_last(n, top, acc):
        if n < 4:
            t = prompt_order[n]
            out = finished(acc)
            for j in range(4):
                for c in range(4):
                    r = j * 64 + c * 16
                    op[4 * t + c, :, j * DH:(j + 1) * DH] = out[r:r + 16]
            for c in range(4):
                g = 4 * t + c
                dst = cut(po, me, QW)

                @pl.when(g != me)
                def _(g=g, c=c, dst=dst):
                    remote(op.at[g], dst, pout_sems.at[g], R_OP,
                           place(t, zh * 2 + c // 2, y, c % 2)).start()

                @pl.when(g == me)
                def _(g=g, dst=dst):
                    pltpu.make_async_copy(op.at[g], dst, recv_sems.at[R_OP]).start()
            if n == 1:
                arrived(own_keys(core, 2), R_A + 2)
                pass_on(own_keys(core, 2), R_ASIB + 3, sibling)
            if n == 2:
                for dy, r in ((0, 0), (-1, 1), (1, 2), (2, 3)):
                    arrived(own_keys(other, dy), R_ASIB + r)
            return
        dx = answer_order[n - 4]
        t = (x + dx) % 4
        out = finished(acc)
        for j in range(4):
            for c in range(4):
                r = j * 128 + c * 32
                oa[4 * t + c, :, j * DH:(j + 1) * DH] = out[r:r + 32]
        dst = cut(ao, me, QW)
        for k in (3, 2, 1, 0):
            d = dx * 4 + k
            g, dev = members[d]
            if d:
                remote(oa.at[g], dst, aout_sems.at[d], R_OA, dev).start()
            else:
                pltpu.make_async_copy(oa.at[g], dst, recv_sems.at[R_OA]).start()

    run_items(last_items, after_last)

    assert len(sends) <= N_SEND
    for copy in sends:
        copy.wait_send()

    @pl.when(core != mine)
    def _():
        for copy in own_sends:
            copy.wait_send()

    for g in range(16):
        @pl.when(g != me)
        def _(g=g):
            pltpu.make_async_copy(op.at[g], op.at[g], pout_sems.at[g]).wait()

    for i in range(1, 16):
        pltpu.make_async_copy(oa.at[i], oa.at[i], aout_sems.at[i]).wait()
    arrived(po, R_OP)
    arrived(ao, R_OA)


def closing(lengths, prompt_in, answer_in, prompt_out, answer_out):
    seq, resp = lax.axis_index("seq"), lax.axis_index("resp")
    height = answer_in.shape[0]
    live = lengths[seq // 2] - (seq % 2) * 256 - resp * height
    prompt_out[...] = prompt_in[...]
    for i in range(0, answer_in.shape[1], 1024):
        rows = lax.broadcasted_iota(jnp.int32, (height, 1024), 0)
        values = answer_in[:, i:i + 1024].astype(jnp.float32)
        answer_out[:, i:i + 1024] = jnp.where(rows < live, values, 0.0).astype(jnp.bfloat16)


def shards(pq, pk, pv, aq, ak, av, answer_lengths):
    bf16, f32 = jnp.bfloat16, jnp.float32
    any_spec = pl.BlockSpec(memory_space=pl.ANY)
    prompt_out, answer_out = pl.pallas_call(
        kernel,
        out_shape=(
            jax.ShapeDtypeStruct(pq.shape, bf16),
            jax.ShapeDtypeStruct(aq.shape, bf16),
        ),
        in_specs=[any_spec] * 6,
        out_specs=(any_spec, any_spec),
        scratch_shapes=[
            pltpu.VMEM((2, 4, 4, 2, 4, 32, DH), bf16),
            pltpu.VMEM((2, 4, 2, 4, 64, DH), bf16),
            pltpu.VMEM((16, 16, QW), bf16),
            pltpu.VMEM((16, 32, QW), bf16),
            pltpu.VMEM((16, 16, QW), bf16),
            pltpu.VMEM((16, 32, QW), bf16),
            pltpu.VMEM((4, 512, 2 * DH), f32),
            pltpu.VMEM((4, 512, DH), f32),
            pltpu.VMEM((6, 512, 512), f32),
            pltpu.VMEM((6, 512, 512), f32),
            pltpu.SemaphoreType.DMA((N_SEND,)),
            pltpu.SemaphoreType.DMA((16,)),
            pltpu.SemaphoreType.DMA((20,)),
            pltpu.SemaphoreType.DMA((N_RECV,)),
        ],
        compiler_params=pltpu.CompilerParams(
            collective_id=0, has_side_effects=True, vmem_limit_bytes=60 * 1024 * 1024),
        cost_estimate=pl.CostEstimate(
            flops=6_400_000_000, bytes_accessed=2_000_000, transcendentals=12_000_000),
    )(pq, pk, pv, aq, ak, av)
    vmem = pl.BlockSpec(memory_space=pltpu.VMEM)
    return pl.pallas_call(
        closing,
        out_shape=(
            jax.ShapeDtypeStruct(pq.shape, bf16),
            jax.ShapeDtypeStruct(aq.shape, bf16),
        ),
        in_specs=[pl.BlockSpec(memory_space=pltpu.SMEM), vmem, vmem],
        out_specs=(vmem, vmem),
        name="closing",
    )(answer_lengths, prompt_out, answer_out)


def solution(mesh):
    rows = P(("prompt", "seq", "resp"), None)
    return jax.shard_map(
        shards,
        mesh=mesh,
        in_specs=(rows,) * 6 + (P("prompt"),),
        out_specs=(rows, rows),
        check_vma=False,
    )
```

```python
import math

import jax
import jax.numpy as jnp
from jax import lax
from jax.experimental import pallas as pl
from jax.experimental.pallas import tpu as pltpu
from jax.sharding import PartitionSpec as P

DH = 128
ZN = 8
QW = 4 * DH
SCALE = math.log2(math.e) / math.sqrt(DH)
BIG_NEG = -1e30
MESH = pl.DeviceIdType.MESH

R_KV, R_AKV, R_QP, R_QA, R_OP, R_OA, R_A = 0, 1, 2, 3, 4, 5, 6
R_FIRST, R_SECOND, R_SIB, R_ASIB = 9, 12, 24, 40
N_RECV = 44
N_SEND = 112
DISTANCES = (0, -1, 1, 2)


def dot_t(a, b):
    return lax.dot_general(a, b, (((1,), (1,)), ((), ())), preferred_element_type=jnp.float32)


def fold_max(s, top):
    for i in range(s.shape[1] // DH):
        c = s[:, i * DH:(i + 1) * DH]
        top = c if top is None else jnp.maximum(top, c)
    return top


def score_piece(item, i, top):
    keys, _values, mask = item.pieces[i]
    s = dot_t(item.q, keys())
    if mask is not None:
        s = jnp.where(mask(), s, BIG_NEG)
    item.buffer(i)[...] = s
    return fold_max(s, top)


def weigh_piece(item, i, top, acc):
    _keys, values, _mask = item.pieces[i]
    p = jnp.exp2((item.buffer(i)[...] - top) * SCALE).astype(jnp.bfloat16)
    v = values()
    v = jnp.concatenate([v, jnp.ones(v.shape, v.dtype)], axis=1)
    part = jnp.dot(p, v, preferred_element_type=jnp.float32)
    return part if acc is None else acc + part


def row_top(folded, old):
    top = jnp.max(folded, axis=1, keepdims=True)
    return top if old is None else jnp.maximum(top, old)


class Item:
    def __init__(self, load, pieces, buffer, state=None):
        self.load, self.pieces, self.buffer, self.state = load, pieces, buffer, state


def run_items(items, between):
    top = None
    for n in range(len(items) + 1):
        new = items[n] if n < len(items) else None
        now = items[n - 1] if n > 0 else None
        folded, acc = None, None
        if new is not None:
            new.q = new.load()
        for i in range(max(len(v.pieces) for v in (new, now) if v is not None)):
            if new is not None and i < len(new.pieces):
                folded = score_piece(new, i, folded)
            if now is not None and i < len(now.pieces):
                acc = weigh_piece(now, i, top, acc)
        if now is not None and now.state is not None:
            old_top, old_acc = now.state()
            acc = acc + old_acc * jnp.exp2((old_top - top) * SCALE)
        now_top = top
        if new is not None:
            top = row_top(folded, None if new.state is None else new.state()[0])
        if now is not None:
            between(n - 1, now_top, acc)


def kernel(pq, pk, pv, aq, ak, av, po, ao, kv, akv, qp, qa, op, oa, accs, tops, s0, s1,
           send_sems, pout_sems, aout_sems, recv_sems):
    part = lax.axis_index("prompt")
    seq = lax.axis_index("seq")
    resp = lax.axis_index("resp")
    x, z = seq // ZN, seq % ZN
    y, core = resp // 2, resp % 2
    zh, zb = z // 2, z % 2
    chip = x * 2 + zb
    me = chip * 2 + core
    mine, other = x // 2, 1 - core

    def place(xx, zz, yy, cc):
        return (part, xx * ZN + zz, yy * 2 + cc)

    def chip_at(dx, dz):
        x2, zb2 = (x + dx) % 4, (zb + dz) % 2
        return x2 * 2 + zb2, x2, zh * 2 + zb2

    def around(v, d):
        return (v + d + 4) % 4

    def first(d):
        return place(x, around(zh, (1 - core) * d) * 2 + zb, around(y, core * d), core)

    def second(d):
        return place(x, around(zh, core * d) * 2 + zb, around(y, (1 - core) * d), core)

    def y_dev(d):
        return place(x, z, around(y, d), core)

    sibling = place(x, z, y, other)
    chips = [chip_at(d // 2, d % 2) for d in range(8)]
    members = [
        (h * 2 + (core + dc) % 2, place(xx, zz, y, (core + dc) % 2))
        for h, xx, zz in chips for dc in range(2)
    ]
    partners = [dev for _, dev in members[1:]] + [first(1), first(-1), first(2), second(1), second(-1)]

    barrier = pltpu.get_barrier_semaphore()
    for dev in partners:
        pl.semaphore_signal(barrier, inc=1, device_id=dev, device_id_type=MESH)

    def cut(ref, h, width):
        return ref.at[:, pl.ds(pl.multiple_of(h * width, width), width)]

    rows_p = pl.ds(pl.multiple_of(core * 16, 16), 16)
    rows_a = pl.ds(pl.multiple_of(core * 32, 32), 32)
    k_land, v_land = kv.at[0, x, zh, zb, y, rows_p], kv.at[1, x, zh, zb, y, rows_p]
    ak_land, av_land = akv.at[0, x, zb, y, rows_a], akv.at[1, x, zb, y, rows_a]

    pltpu.make_async_copy(cut(pq, me, QW), qp.at[me], recv_sems.at[R_QP]).start()
    pltpu.make_async_copy(cut(aq, me, QW), qa.at[me], recv_sems.at[R_QA]).start()
    own_parts = (
        (cut(pk, chip, DH), k_land, R_KV), (cut(pv, chip, DH), v_land, R_KV),
        (cut(ak, chip, DH), ak_land, R_AKV), (cut(av, chip, DH), av_land, R_AKV))

    @pl.when(core == mine)
    def _():
        for src, dst, r in own_parts:
            pltpu.make_async_copy(src, dst, recv_sems.at[r]).start()

    pl.semaphore_wait(barrier, len(partners))

    sends = []

    def remote(src, dst, send_sem, r, dev):
        return pltpu.make_async_remote_copy(
            src_ref=src, dst_ref=dst, send_sem=send_sem,
            recv_sem=recv_sems.at[r], device_id=dev, device_id_type=MESH)

    def send(src, dst, r, dev):
        copy = remote(src, dst, send_sems.at[len(sends)], r, dev)
        copy.start()
        sends.append(copy)

    def pass_on(ref, r, dev):
        send(ref, ref, r, dev)

    def arrived(ref, r):
        pltpu.make_async_copy(ref, ref, recv_sems.at[r]).wait()

    own_sends = [remote(src, dst, aout_sems.at[1 + i], r, sibling)
                 for i, (src, dst, r) in enumerate(own_parts)]

    def part_of(c, d1, d2, n=slice(None)):
        zz = around(zh, (1 - c) * d1 + c * d2)
        yy = around(y, (1 - c) * d2 + c * d1)
        return kv.at[n, pl.ds(2 * c, 2), zz, :, yy]

    def shard(d1, d2):
        return part_of(core, d1, d2)

    def to_sibling(d1, d2):
        k = DISTANCES.index(d2) * 4 + DISTANCES.index(d1)
        pass_on(shard(d1, d2), R_SIB + k, sibling)

    def from_sibling(d1, d2):
        k = DISTANCES.index(d2) * 4 + DISTANCES.index(d1)
        arrived(part_of(other, d1, d2), R_SIB + k)

    def start_first():
        for k, d in enumerate((1, -1, 2)):
            pass_on(shard(0, 0), R_FIRST + k, first(d))

    def start_second(d1):
        r = R_SECOND + 3 * DISTANCES.index(d1)
        pass_on(shard(d1, 0), r, second(1))
        pass_on(shard(d1, 0), r + 1, second(-1))

    def middle_second(d1):
        r = R_SECOND + 3 * DISTANCES.index(d1)
        arrived(shard(d1, -1), r)
        pass_on(part_of(core, d1, -1, 0), r + 2, second(1))
        arrived(shard(d1, 1), r + 1)
        pass_on(part_of(core, d1, 1, 1), r + 2, second(-1))
        to_sibling(d1, -1)
        to_sibling(d1, 1)

    def hand_over(d1):
        arrived(shard(d1, 2), R_SECOND + 3 * DISTANCES.index(d1) + 2)
        to_sibling(d1, 2)

    def own_keys(c, dy, n=slice(None)):
        return akv.at[n, pl.ds(2 * c, 2), :, around(y, dy)]

    for d in (7, 6, 5, 4, 3, 2, 1):
        h, xx, zz = chips[d]
        send(cut(pk, h, DH), k_land, R_KV, place(xx, zz, y, mine))
        send(cut(pv, h, DH), v_land, R_KV, place(xx, zz, y, mine))

    @pl.when(core != mine)
    def _():
        for copy in own_sends:
            copy.start()

    for d in (7, 6, 5, 4, 3, 2, 1):
        h, xx, zz = chips[d]
        send(cut(ak, h, DH), ak_land, R_AKV, place(xx, zz, y, mine))
        send(cut(av, h, DH), av_land, R_AKV, place(xx, zz, y, mine))
    arrived(shard(0, 0), R_KV)
    start_first()
    start_second(0)
    to_sibling(0, 0)
    arrived(own_keys(core, 0), R_AKV)
    pass_on(own_keys(core, 0), R_A, y_dev(1))
    pass_on(own_keys(core, 0), R_A + 1, y_dev(-1))
    pass_on(own_keys(core, 0), R_ASIB, sibling)
    for g, dev in members[:0:-1]:
        send(cut(aq, g, QW), qa.at[me], R_QA, dev)
    for k, d1 in enumerate((-1, 1, 2)):
        arrived(shard(d1, 0), R_FIRST + k)
        start_second(d1)
        to_sibling(d1, 0)
    for g, dev in members[:0:-1]:
        send(cut(pq, g, QW), qp.at[me], R_QP, dev)

    bufs = (s0, s1)

    def low(dy):
        def take(n):
            return kv[n, 0:2, :, :, around(y, dy)].reshape(512, DH)
        return (lambda: take(0), lambda: take(1), None)

    def high(dz):
        def take(n):
            return kv[n, 2:4, around(zh, dz)].reshape(512, DH)
        return (lambda: take(0), lambda: take(1), None)

    def half_slab(xx, h, mask=None):
        def take(n):
            return kv[n, xx, 2 * h:2 * h + 2].reshape(512, DH)
        return (lambda: take(0), lambda: take(1), mask)

    def iota(height, axis):
        return lax.broadcasted_iota(jnp.int32, (height, 512), axis)

    def answer_tile(t):
        return jnp.concatenate(
            [qa[4 * t + c, :, j * DH:(j + 1) * DH] for j in range(4) for c in range(4)], axis=0)

    def prompt_tile(t):
        return jnp.concatenate(
            [qp[4 * t + c, :, j * DH:(j + 1) * DH] for j in range(4) for c in range(4)], axis=0)

    def wide(b):
        return lambda i: bufs[b].at[i]

    def tall(b):
        return lambda i: bufs[b].at[i // 2, (i % 2) * 256:(i % 2) * 256 + 256]

    def keep(n, top, acc):
        tops[n] = jnp.broadcast_to(top, (512, DH))
        accs[n] = acc

    def kept(t):
        return tops[t][:, :1], accs[t]

    early = len(sends)

    for d1 in DISTANCES:
        from_sibling(d1, 0)
    arrived(qa, R_QA)
    run_items([
        Item(lambda t=t: answer_tile(t), [low(0), high(0)], wide(t % 2)) for t in range(4)
    ], keep)

    for d1 in DISTANCES:
        middle_second(d1)
    arrived(own_keys(core, -1), R_A)
    pass_on(own_keys(core, -1, 0), R_A + 2, y_dev(1))
    arrived(own_keys(core, 1), R_A + 1)
    pass_on(own_keys(core, 1, 1), R_A + 2, y_dev(-1))
    pass_on(own_keys(core, -1), R_ASIB + 1, sibling)
    pass_on(own_keys(core, 1), R_ASIB + 2, sibling)
    for copy in sends[:early]:
        copy.wait_send()
    for d2 in (-1, 1):
        for d1 in DISTANCES:
            from_sibling(d1, d2)

    def after_second(n, top, acc):
        keep(n, top, acc)
        if n == 2:
            for d1 in DISTANCES:
                hand_over(d1)
            arrived(own_keys(core, 2), R_A + 2)
            pass_on(own_keys(core, 2), R_ASIB + 3, sibling)

    run_items([
        Item(lambda t=t: answer_tile(t), [f(d) for d in (-1, 1) for f in (low, high)],
             wide(t % 2), lambda t=t: kept(t))
        for t in range(4)
    ], after_second)

    for d1 in DISTANCES:
        from_sibling(d1, 2)
    arrived(qp, R_QP)
    for dy, r in ((0, 0), (-1, 1), (1, 2), (2, 3)):
        arrived(own_keys(other, dy), R_ASIB + r)

    def prompt_mask(h):
        rows = iota(256, 0)
        here = (2 * zh) * 128 + y * 32 + ((rows // 32) % 2) * 128 + rows % 32
        return iota(256, 1) + h * 512 <= here

    def answer_mask():
        rows = iota(512, 0)
        return iota(512, 1) <= ((rows // 64) % 2) * 256 + y * 64 + rows % 64

    prompt_order = (3, 2, 1, 0)
    answer_order = (2, 1, 3, 0)
    last_items = []
    for dx in answer_order:
        t = (x + dx) % 4
        own_piece = (
            lambda t=t: akv[0, t].reshape(512, DH), lambda t=t: akv[1, t].reshape(512, DH),
            answer_mask)
        last_items.append(Item(
            lambda t=t: answer_tile(t), [low(2), high(2), own_piece], wide(len(last_items) % 2),
            lambda t=t: kept(t)))
    for t in prompt_order:
        pieces = [half_slab(i, h) for i in range(t) for h in range(2)]
        pieces += [half_slab(t, h, lambda h=h: prompt_mask(h)) for h in range(2)]
        last_items.append(Item(lambda t=t: prompt_tile(t), pieces, tall(len(last_items) % 2)))

    def finished(acc):
        return (acc[:, :DH] / acc[:, DH:]).astype(jnp.bfloat16)

    def after_last(n, top, acc):
        if n >= 4:
            t = prompt_order[n - 4]
            out = finished(acc)
            for j in range(4):
                for c in range(4):
                    r = j * 64 + c * 16
                    op[4 * t + c, :, j * DH:(j + 1) * DH] = out[r:r + 16]
            for c in range(4):
                g = 4 * t + c
                dst = cut(po, me, QW)

                @pl.when(g != me)
                def _(g=g, c=c, dst=dst):
                    remote(op.at[g], dst, pout_sems.at[0], R_OP,
                           place(t, zh * 2 + c // 2, y, c % 2)).start()

                @pl.when(g == me)
                def _(g=g, dst=dst):
                    pltpu.make_async_copy(op.at[g], dst, recv_sems.at[R_OP]).start()
            return
        dx = answer_order[n]
        t = (x + dx) % 4
        out = finished(acc)
        for j in range(4):
            for c in range(4):
                r = j * 128 + c * 32
                oa[4 * t + c, :, j * DH:(j + 1) * DH] = out[r:r + 32]
        dst = cut(ao, me, QW)
        for k in (3, 2, 1, 0):
            d = dx * 4 + k
            g, dev = members[d]
            if d:
                remote(oa.at[g], dst, aout_sems.at[0], R_OA, dev).start()
            else:
                pltpu.make_async_copy(oa.at[g], dst, recv_sems.at[R_OA]).start()

    run_items(last_items, after_last)

    assert len(sends) <= N_SEND
    for copy in sends[early:]:
        copy.wait_send()

    @pl.when(core != mine)
    def _():
        for copy in own_sends:
            copy.wait_send()

    pltpu.make_async_copy(op.at[0:15], op.at[0:15], pout_sems.at[0]).wait()
    pltpu.make_async_copy(oa.at[0:15], oa.at[0:15], aout_sems.at[0]).wait()
    arrived(po, R_OP)
    arrived(ao, R_OA)


def closing(lengths, prompt_in, answer_in, prompt_out, answer_out):
    seq, resp = lax.axis_index("seq"), lax.axis_index("resp")
    height = answer_in.shape[0]
    live = lengths[seq // 2] - (seq % 2) * 256 - resp * height
    prompt_out[...] = prompt_in[...]
    for i in range(0, answer_in.shape[1], 1024):
        rows = lax.broadcasted_iota(jnp.int32, (height, 1024), 0)
        values = answer_in[:, i:i + 1024].astype(jnp.float32)
        answer_out[:, i:i + 1024] = jnp.where(rows < live, values, 0.0).astype(jnp.bfloat16)


def shards(pq, pk, pv, aq, ak, av, answer_lengths):
    bf16, f32 = jnp.bfloat16, jnp.float32
    any_spec = pl.BlockSpec(memory_space=pl.ANY)
    prompt_out, answer_out = pl.pallas_call(
        kernel,
        out_shape=(
            jax.ShapeDtypeStruct(pq.shape, bf16),
            jax.ShapeDtypeStruct(aq.shape, bf16),
        ),
        in_specs=[any_spec] * 6,
        out_specs=(any_spec, any_spec),
        scratch_shapes=[
            pltpu.VMEM((2, 4, 4, 2, 4, 32, DH), bf16),
            pltpu.VMEM((2, 4, 2, 4, 64, DH), bf16),
            pltpu.VMEM((16, 16, QW), bf16),
            pltpu.VMEM((16, 32, QW), bf16),
            pltpu.VMEM((16, 16, QW), bf16),
            pltpu.VMEM((16, 32, QW), bf16),
            pltpu.VMEM((4, 512, 2 * DH), f32),
            pltpu.VMEM((4, 512, DH), f32),
            pltpu.VMEM((6, 512, 512), f32),
            pltpu.VMEM((6, 512, 512), f32),
            pltpu.SemaphoreType.DMA((N_SEND,)),
            pltpu.SemaphoreType.DMA((1,)),
            pltpu.SemaphoreType.DMA((5,)),
            pltpu.SemaphoreType.DMA((N_RECV,)),
        ],
        compiler_params=pltpu.CompilerParams(
            collective_id=0, has_side_effects=True, vmem_limit_bytes=60 * 1024 * 1024),
        cost_estimate=pl.CostEstimate(
            flops=6_400_000_000, bytes_accessed=2_000_000, transcendentals=12_000_000),
    )(pq, pk, pv, aq, ak, av)
    vmem = pl.BlockSpec(memory_space=pltpu.VMEM)
    return pl.pallas_call(
        closing,
        out_shape=(
            jax.ShapeDtypeStruct(pq.shape, bf16),
            jax.ShapeDtypeStruct(aq.shape, bf16),
        ),
        in_specs=[pl.BlockSpec(memory_space=pltpu.SMEM), vmem, vmem],
        out_specs=(vmem, vmem),
        name="closing",
    )(answer_lengths, prompt_out, answer_out)


def solution(mesh):
    rows = P(("prompt", "seq", "resp"), None)
    return jax.shard_map(
        shards,
        mesh=mesh,
        in_specs=(rows,) * 6 + (P("prompt"),),
        out_specs=(rows, rows),
        check_vma=False,
    )
```

```python
import math

import jax
import jax.numpy as jnp
from jax import lax
from jax.experimental import pallas as pl
from jax.experimental.pallas import tpu as pltpu
from jax.sharding import PartitionSpec as P

DH = 128
ZN = 8
QW = 4 * DH
SCALE = math.log2(math.e) / math.sqrt(DH)
BIG_NEG = -1e30
MESH = pl.DeviceIdType.MESH

R_KV, R_AKV, R_QP, R_QA, R_OP, R_OA, R_A = 0, 1, 2, 3, 4, 5, 6
R_FIRST, R_SECOND, R_SIB, R_ASIB = 9, 12, 24, 40
N_RECV = 44
N_SEND = 112
DISTANCES = (0, -1, 1, 2)


def dot_t(a, b):
    return lax.dot_general(a, b, (((1,), (1,)), ((), ())), preferred_element_type=jnp.float32)


def fold_max(s, top):
    for i in range(s.shape[1] // DH):
        c = s[:, i * DH:(i + 1) * DH]
        top = c if top is None else jnp.maximum(top, c)
    return top


def score_piece(item, i, top):
    keys, _values, mask = item.pieces[i]
    s = dot_t(item.q, keys())
    if mask is not None:
        s = jnp.where(mask(), s, BIG_NEG)
    item.buffer(i)[...] = s
    return fold_max(s, top)


def weigh_piece(item, i, top, acc):
    _keys, values, _mask = item.pieces[i]
    p = jnp.exp2((item.buffer(i)[...] - top) * SCALE).astype(jnp.bfloat16)
    v = values()
    v = jnp.concatenate([v, jnp.ones(v.shape, v.dtype)], axis=1)
    part = jnp.dot(p, v, preferred_element_type=jnp.float32)
    return part if acc is None else acc + part


def row_top(folded, old):
    top = jnp.max(folded, axis=1, keepdims=True)
    return top if old is None else jnp.maximum(top, old)


class Item:
    def __init__(self, load, pieces, buffer, state=None):
        self.load, self.pieces, self.buffer, self.state = load, pieces, buffer, state


def run_items(items, between):
    top = None
    for n in range(len(items) + 1):
        new = items[n] if n < len(items) else None
        now = items[n - 1] if n > 0 else None
        folded, acc = None, None
        if new is not None:
            new.q = new.load()
        for i in range(max(len(v.pieces) for v in (new, now) if v is not None)):
            if new is not None and i < len(new.pieces):
                folded = score_piece(new, i, folded)
            if now is not None and i < len(now.pieces):
                acc = weigh_piece(now, i, top, acc)
        if now is not None and now.state is not None:
            old_top, old_acc = now.state()
            acc = acc + old_acc * jnp.exp2((old_top - top) * SCALE)
        now_top = top
        if new is not None:
            top = row_top(folded, None if new.state is None else new.state()[0])
        if now is not None:
            between(n - 1, now_top, acc)


def kernel(pq, pk, pv, aq, ak, av, po, ao, kv, akv, qp, qa, op, oa, accs, tops, s0, s1,
           send_sems, pout_sems, aout_sems, recv_sems):
    part = lax.axis_index("prompt")
    seq = lax.axis_index("seq")
    resp = lax.axis_index("resp")
    x, z = seq // ZN, seq % ZN
    y, core = resp // 2, resp % 2
    zh, zb = z // 2, z % 2
    chip = x * 2 + zb
    me = chip * 2 + core
    mine, other = x // 2, 1 - core

    def place(xx, zz, yy, cc):
        return (part, xx * ZN + zz, yy * 2 + cc)

    def chip_at(dx, dz):
        x2, zb2 = (x + dx) % 4, (zb + dz) % 2
        return x2 * 2 + zb2, x2, zh * 2 + zb2

    def around(v, d):
        return (v + d + 4) % 4

    def first(d):
        return place(x, around(zh, (1 - core) * d) * 2 + zb, around(y, core * d), core)

    def second(d):
        return place(x, around(zh, core * d) * 2 + zb, around(y, (1 - core) * d), core)

    def y_dev(d):
        return place(x, z, around(y, d), core)

    sibling = place(x, z, y, other)
    chips = [chip_at(d // 2, d % 2) for d in range(8)]
    members = [
        (h * 2 + (core + dc) % 2, place(xx, zz, y, (core + dc) % 2))
        for h, xx, zz in chips for dc in range(2)
    ]
    partners = [dev for _, dev in members[1:]] + [first(1), first(-1), first(2), second(1), second(-1)]

    barrier = pltpu.get_barrier_semaphore()
    for dev in partners:
        pl.semaphore_signal(barrier, inc=1, device_id=dev, device_id_type=MESH)

    def cut(ref, h, width):
        return ref.at[:, pl.ds(pl.multiple_of(h * width, width), width)]

    rows_p = pl.ds(pl.multiple_of(core * 16, 16), 16)
    rows_a = pl.ds(pl.multiple_of(core * 32, 32), 32)
    k_land, v_land = kv.at[0, x, zh, zb, y, rows_p], kv.at[1, x, zh, zb, y, rows_p]
    ak_land, av_land = akv.at[0, x, zb, y, rows_a], akv.at[1, x, zb, y, rows_a]

    pltpu.make_async_copy(cut(pq, me, QW), qp.at[me], recv_sems.at[R_QP]).start()
    pltpu.make_async_copy(cut(aq, me, QW), qa.at[me], recv_sems.at[R_QA]).start()
    own_parts = (
        (cut(pk, chip, DH), k_land, R_KV), (cut(pv, chip, DH), v_land, R_KV),
        (cut(ak, chip, DH), ak_land, R_AKV), (cut(av, chip, DH), av_land, R_AKV))

    @pl.when(core == mine)
    def _():
        for src, dst, r in own_parts:
            pltpu.make_async_copy(src, dst, recv_sems.at[r]).start()

    pl.semaphore_wait(barrier, len(partners))

    sends = []

    def remote(src, dst, send_sem, r, dev):
        return pltpu.make_async_remote_copy(
            src_ref=src, dst_ref=dst, send_sem=send_sem,
            recv_sem=recv_sems.at[r], device_id=dev, device_id_type=MESH)

    def send(src, dst, r, dev):
        copy = remote(src, dst, send_sems.at[len(sends)], r, dev)
        copy.start()
        sends.append(copy)

    def pass_on(ref, r, dev):
        send(ref, ref, r, dev)

    def arrived(ref, r):
        pltpu.make_async_copy(ref, ref, recv_sems.at[r]).wait()

    own_sends = [remote(src, dst, aout_sems.at[1 + i], r, sibling)
                 for i, (src, dst, r) in enumerate(own_parts)]

    def part_of(c, d1, d2, n=slice(None)):
        zz = around(zh, (1 - c) * d1 + c * d2)
        yy = around(y, (1 - c) * d2 + c * d1)
        return kv.at[n, pl.ds(2 * c, 2), zz, :, yy]

    def shard(d1, d2):
        return part_of(core, d1, d2)

    def to_sibling(d1, d2):
        k = DISTANCES.index(d2) * 4 + DISTANCES.index(d1)
        pass_on(shard(d1, d2), R_SIB + k, sibling)

    def from_sibling(d1, d2):
        k = DISTANCES.index(d2) * 4 + DISTANCES.index(d1)
        arrived(part_of(other, d1, d2), R_SIB + k)

    def start_first():
        for k, d in enumerate((1, -1, 2)):
            pass_on(shard(0, 0), R_FIRST + k, first(d))

    def start_second(d1):
        r = R_SECOND + 3 * DISTANCES.index(d1)
        pass_on(shard(d1, 0), r, second(1))
        pass_on(shard(d1, 0), r + 1, second(-1))

    def middle_second(d1):
        r = R_SECOND + 3 * DISTANCES.index(d1)
        arrived(shard(d1, -1), r)
        pass_on(part_of(core, d1, -1, 0), r + 2, second(1))
        arrived(shard(d1, 1), r + 1)
        pass_on(part_of(core, d1, 1, 1), r + 2, second(-1))
        to_sibling(d1, -1)
        to_sibling(d1, 1)

    def hand_over(d1):
        arrived(shard(d1, 2), R_SECOND + 3 * DISTANCES.index(d1) + 2)
        to_sibling(d1, 2)

    def own_keys(c, dy, n=slice(None)):
        return akv.at[n, pl.ds(2 * c, 2), :, around(y, dy)]

    for d in (7, 6, 5, 4, 3, 2, 1):
        h, xx, zz = chips[d]
        send(cut(pk, h, DH), k_land, R_KV, place(xx, zz, y, mine))
        send(cut(pv, h, DH), v_land, R_KV, place(xx, zz, y, mine))

    @pl.when(core != mine)
    def _():
        for copy in own_sends:
            copy.start()

    for d in (7, 6, 5, 4, 3, 2, 1):
        h, xx, zz = chips[d]
        send(cut(ak, h, DH), ak_land, R_AKV, place(xx, zz, y, mine))
        send(cut(av, h, DH), av_land, R_AKV, place(xx, zz, y, mine))
    arrived(shard(0, 0), R_KV)
    start_first()
    start_second(0)
    to_sibling(0, 0)
    arrived(own_keys(core, 0), R_AKV)
    pass_on(own_keys(core, 0), R_A, y_dev(1))
    pass_on(own_keys(core, 0), R_A + 1, y_dev(-1))
    pass_on(own_keys(core, 0), R_ASIB, sibling)
    for g, dev in members[:0:-1]:
        send(cut(aq, g, QW), qa.at[me], R_QA, dev)
    for k, d1 in enumerate((-1, 1, 2)):
        arrived(shard(d1, 0), R_FIRST + k)
        start_second(d1)
        to_sibling(d1, 0)

    bufs = (s0, s1)

    def low(dy):
        def take(n):
            return kv[n, 0:2, :, :, around(y, dy)].reshape(512, DH)
        return (lambda: take(0), lambda: take(1), None)

    def high(dz):
        def take(n):
            return kv[n, 2:4, around(zh, dz)].reshape(512, DH)
        return (lambda: take(0), lambda: take(1), None)

    def half_slab(xx, h, mask=None):
        def take(n):
            return kv[n, xx, 2 * h:2 * h + 2].reshape(512, DH)
        return (lambda: take(0), lambda: take(1), mask)

    def iota(height, axis):
        return lax.broadcasted_iota(jnp.int32, (height, 512), axis)

    def answer_tile(t):
        return jnp.concatenate(
            [qa[4 * t + c, :, j * DH:(j + 1) * DH] for j in range(4) for c in range(4)], axis=0)

    def prompt_tile(t):
        return jnp.concatenate(
            [qp[4 * t + c, :, j * DH:(j + 1) * DH] for j in range(4) for c in range(4)], axis=0)

    def wide(b):
        return lambda i: bufs[b].at[i]

    def tall(b):
        return lambda i: bufs[b].at[i // 2, (i % 2) * 256:(i % 2) * 256 + 256]

    def keep(n, top, acc):
        tops[n] = jnp.broadcast_to(top, (512, DH))
        accs[n] = acc

    def kept(t):
        return tops[t][:, :1], accs[t]

    early = len(sends)

    for d1 in DISTANCES:
        from_sibling(d1, 0)
    arrived(qa, R_QA)
    run_items([
        Item(lambda t=t: answer_tile(t), [low(0), high(0)], wide(t % 2)) for t in range(4)
    ], keep)

    for d1 in DISTANCES:
        middle_second(d1)
    arrived(own_keys(core, -1), R_A)
    pass_on(own_keys(core, -1, 0), R_A + 2, y_dev(1))
    arrived(own_keys(core, 1), R_A + 1)
    pass_on(own_keys(core, 1, 1), R_A + 2, y_dev(-1))
    pass_on(own_keys(core, -1), R_ASIB + 1, sibling)
    pass_on(own_keys(core, 1), R_ASIB + 2, sibling)
    for g, dev in members[:0:-1]:
        send(cut(pq, g, QW), qp.at[me], R_QP, dev)
    for copy in sends[:early]:
        copy.wait_send()
    for d2 in (-1, 1):
        for d1 in DISTANCES:
            from_sibling(d1, d2)

    def after_second(n, top, acc):
        keep(n, top, acc)
        if n == 2:
            for d1 in DISTANCES:
                hand_over(d1)
            arrived(own_keys(core, 2), R_A + 2)
            pass_on(own_keys(core, 2), R_ASIB + 3, sibling)

    run_items([
        Item(lambda t=t: answer_tile(t), [f(d) for d in (-1, 1) for f in (low, high)],
             wide(t % 2), lambda t=t: kept(t))
        for t in range(4)
    ], after_second)

    for d1 in DISTANCES:
        from_sibling(d1, 2)
    for dy, r in ((0, 0), (-1, 1), (1, 2), (2, 3)):
        arrived(own_keys(other, dy), R_ASIB + r)

    def prompt_mask(h):
        rows = iota(256, 0)
        here = (2 * zh) * 128 + y * 32 + ((rows // 32) % 2) * 128 + rows % 32
        return iota(256, 1) + h * 512 <= here

    def answer_mask():
        rows = iota(512, 0)
        return iota(512, 1) <= ((rows // 64) % 2) * 256 + y * 64 + rows % 64

    prompt_order = (3, 2, 1, 0)
    answer_order = (2, 1, 3, 0)
    last_items = []
    for dx in answer_order:
        t = (x + dx) % 4
        own_piece = (
            lambda t=t: akv[0, t].reshape(512, DH), lambda t=t: akv[1, t].reshape(512, DH),
            answer_mask)
        last_items.append(Item(
            lambda t=t: answer_tile(t), [low(2), high(2), own_piece], wide(len(last_items) % 2),
            lambda t=t: kept(t)))
    for t in prompt_order:
        pieces = [half_slab(i, h) for i in range(t) for h in range(2)]
        pieces += [half_slab(t, h, lambda h=h: prompt_mask(h)) for h in range(2)]
        last_items.append(Item(lambda t=t: prompt_tile(t), pieces, tall(len(last_items) % 2)))

    def finished(acc):
        return (acc[:, :DH] / acc[:, DH:]).astype(jnp.bfloat16)

    def after_last(n, top, acc):
        if n == 2:
            arrived(qp, R_QP)
        if n >= 4:
            t = prompt_order[n - 4]
            out = finished(acc)
            for j in range(4):
                for c in range(4):
                    r = j * 64 + c * 16
                    op[4 * t + c, :, j * DH:(j + 1) * DH] = out[r:r + 16]
            for c in range(4):
                g = 4 * t + c
                dst = cut(po, me, QW)

                @pl.when(g != me)
                def _(g=g, c=c, dst=dst):
                    remote(op.at[g], dst, pout_sems.at[0], R_OP,
                           place(t, zh * 2 + c // 2, y, c % 2)).start()

                @pl.when(g == me)
                def _(g=g, dst=dst):
                    pltpu.make_async_copy(op.at[g], dst, recv_sems.at[R_OP]).start()
            return
        dx = answer_order[n]
        t = (x + dx) % 4
        out = finished(acc)
        for j in range(4):
            for c in range(4):
                r = j * 128 + c * 32
                oa[4 * t + c, :, j * DH:(j + 1) * DH] = out[r:r + 32]
        dst = cut(ao, me, QW)
        for k in (3, 2, 1, 0):
            d = dx * 4 + k
            g, dev = members[d]
            if d:
                remote(oa.at[g], dst, aout_sems.at[0], R_OA, dev).start()
            else:
                pltpu.make_async_copy(oa.at[g], dst, recv_sems.at[R_OA]).start()

    run_items(last_items, after_last)

    assert len(sends) <= N_SEND
    for copy in sends[early:]:
        copy.wait_send()

    @pl.when(core != mine)
    def _():
        for copy in own_sends:
            copy.wait_send()

    pltpu.make_async_copy(op.at[0:15], op.at[0:15], pout_sems.at[0]).wait()
    pltpu.make_async_copy(oa.at[0:15], oa.at[0:15], aout_sems.at[0]).wait()
    arrived(po, R_OP)
    arrived(ao, R_OA)


def closing(lengths, prompt_in, answer_in, prompt_out, answer_out):
    seq, resp = lax.axis_index("seq"), lax.axis_index("resp")
    height = answer_in.shape[0]
    live = lengths[seq // 2] - (seq % 2) * 256 - resp * height
    prompt_out[...] = prompt_in[...]
    for i in range(0, answer_in.shape[1], 1024):
        rows = lax.broadcasted_iota(jnp.int32, (height, 1024), 0)
        values = answer_in[:, i:i + 1024].astype(jnp.float32)
        answer_out[:, i:i + 1024] = jnp.where(rows < live, values, 0.0).astype(jnp.bfloat16)


def shards(pq, pk, pv, aq, ak, av, answer_lengths):
    bf16, f32 = jnp.bfloat16, jnp.float32
    any_spec = pl.BlockSpec(memory_space=pl.ANY)
    prompt_out, answer_out = pl.pallas_call(
        kernel,
        out_shape=(
            jax.ShapeDtypeStruct(pq.shape, bf16),
            jax.ShapeDtypeStruct(aq.shape, bf16),
        ),
        in_specs=[any_spec] * 6,
        out_specs=(any_spec, any_spec),
        scratch_shapes=[
            pltpu.VMEM((2, 4, 4, 2, 4, 32, DH), bf16),
            pltpu.VMEM((2, 4, 2, 4, 64, DH), bf16),
            pltpu.VMEM((16, 16, QW), bf16),
            pltpu.VMEM((16, 32, QW), bf16),
            pltpu.VMEM((16, 16, QW), bf16),
            pltpu.VMEM((16, 32, QW), bf16),
            pltpu.VMEM((4, 512, 2 * DH), f32),
            pltpu.VMEM((4, 512, DH), f32),
            pltpu.VMEM((6, 512, 512), f32),
            pltpu.VMEM((6, 512, 512), f32),
            pltpu.SemaphoreType.DMA((N_SEND,)),
            pltpu.SemaphoreType.DMA((1,)),
            pltpu.SemaphoreType.DMA((5,)),
            pltpu.SemaphoreType.DMA((N_RECV,)),
        ],
        compiler_params=pltpu.CompilerParams(
            collective_id=0, has_side_effects=True, vmem_limit_bytes=60 * 1024 * 1024),
        cost_estimate=pl.CostEstimate(
            flops=6_400_000_000, bytes_accessed=2_000_000, transcendentals=12_000_000),
    )(pq, pk, pv, aq, ak, av)
    vmem = pl.BlockSpec(memory_space=pltpu.VMEM)
    return pl.pallas_call(
        closing,
        out_shape=(
            jax.ShapeDtypeStruct(pq.shape, bf16),
            jax.ShapeDtypeStruct(aq.shape, bf16),
        ),
        in_specs=[pl.BlockSpec(memory_space=pltpu.SMEM), vmem, vmem],
        out_specs=(vmem, vmem),
        name="closing",
    )(answer_lengths, prompt_out, answer_out)


def solution(mesh):
    rows = P(("prompt", "seq", "resp"), None)
    return jax.shard_map(
        shards,
        mesh=mesh,
        in_specs=(rows,) * 6 + (P("prompt"),),
        out_specs=(rows, rows),
        check_vma=False,
    )
```

```python
import math

import jax
import jax.numpy as jnp
from jax import lax
from jax.experimental import pallas as pl
from jax.experimental.pallas import tpu as pltpu
from jax.sharding import PartitionSpec as P

DH = 128
ZN = 8
QW = 4 * DH
SCALE = math.log2(math.e) / math.sqrt(DH)
BIG_NEG = -1e30
MESH = pl.DeviceIdType.MESH

R_KV, R_AKV, R_QP, R_QA, R_OP, R_OA, R_A = 0, 1, 2, 3, 4, 5, 6
R_FIRST, R_SECOND, R_SIB, R_ASIB = 9, 12, 24, 40
N_RECV = 44
N_SEND = 112
DISTANCES = (0, -1, 1, 2)


def dot_t(a, b):
    return lax.dot_general(a, b, (((1,), (1,)), ((), ())), preferred_element_type=jnp.float32)


def fold_max(s, top):
    for i in range(s.shape[1] // DH):
        c = s[:, i * DH:(i + 1) * DH]
        top = c if top is None else jnp.maximum(top, c)
    return top


def score_piece(item, i, top):
    keys, _values, mask = item.pieces[i]
    s = dot_t(item.q, keys())
    if mask is not None:
        s = jnp.where(mask(), s, BIG_NEG)
    item.buffer(i)[...] = s
    return fold_max(s, top)


def weigh_piece(item, i, top, acc):
    _keys, values, _mask = item.pieces[i]
    p = jnp.exp2((item.buffer(i)[...] - top) * SCALE).astype(jnp.bfloat16)
    v = values()
    v = jnp.concatenate([v, jnp.ones(v.shape, v.dtype)], axis=1)
    part = jnp.dot(p, v, preferred_element_type=jnp.float32)
    return part if acc is None else acc + part


def row_top(folded, old):
    top = jnp.max(folded, axis=1, keepdims=True)
    return top if old is None else jnp.maximum(top, old)


class Item:
    def __init__(self, load, pieces, buffer, state=None):
        self.load, self.pieces, self.buffer, self.state = load, pieces, buffer, state


def run_items(items, between):
    top = None
    for n in range(len(items) + 1):
        new = items[n] if n < len(items) else None
        now = items[n - 1] if n > 0 else None
        folded, acc = None, None
        if new is not None:
            new.q = new.load()
        for i in range(max(len(v.pieces) for v in (new, now) if v is not None)):
            if new is not None and i < len(new.pieces):
                folded = score_piece(new, i, folded)
            if now is not None and i < len(now.pieces):
                acc = weigh_piece(now, i, top, acc)
        if now is not None and now.state is not None:
            old_top, old_acc = now.state()
            acc = acc + old_acc * jnp.exp2((old_top - top) * SCALE)
        now_top = top
        if new is not None:
            top = row_top(folded, None if new.state is None else new.state()[0])
        if now is not None:
            between(n - 1, now_top, acc)


def kernel(pq, pk, pv, aq, ak, av, po, ao, kv, akv, qp, qa, op, oa, accs, tops, s0, s1,
           send_sems, pout_sems, aout_sems, recv_sems):
    part = lax.axis_index("prompt")
    seq = lax.axis_index("seq")
    resp = lax.axis_index("resp")
    x, z = seq // ZN, seq % ZN
    y, core = resp // 2, resp % 2
    zh, zb = z // 2, z % 2
    chip = x * 2 + zb
    me = chip * 2 + core
    mine, other = x // 2, 1 - core

    def place(xx, zz, yy, cc):
        return (part, xx * ZN + zz, yy * 2 + cc)

    def chip_at(dx, dz):
        x2, zb2 = (x + dx) % 4, (zb + dz) % 2
        return x2 * 2 + zb2, x2, zh * 2 + zb2

    def around(v, d):
        return (v + d + 4) % 4

    def first(d):
        return place(x, around(zh, (1 - core) * d) * 2 + zb, around(y, core * d), core)

    def second(d):
        return place(x, around(zh, core * d) * 2 + zb, around(y, (1 - core) * d), core)

    def y_dev(d):
        return place(x, z, around(y, d), core)

    sibling = place(x, z, y, other)
    chips = [chip_at(d // 2, d % 2) for d in range(8)]
    members = [
        (h * 2 + (core + dc) % 2, place(xx, zz, y, (core + dc) % 2))
        for h, xx, zz in chips for dc in range(2)
    ]
    partners = [dev for _, dev in members[1:]] + [first(1), first(-1), first(2), second(1), second(-1)]

    barrier = pltpu.get_barrier_semaphore()
    for dev in partners:
        pl.semaphore_signal(barrier, inc=1, device_id=dev, device_id_type=MESH)

    def cut(ref, h, width):
        return ref.at[:, pl.ds(pl.multiple_of(h * width, width), width)]

    rows_p = pl.ds(pl.multiple_of(core * 16, 16), 16)
    rows_a = pl.ds(pl.multiple_of(core * 32, 32), 32)
    k_land, v_land = kv.at[0, x, zh, zb, y, rows_p], kv.at[1, x, zh, zb, y, rows_p]
    ak_land, av_land = akv.at[0, x, zb, y, rows_a], akv.at[1, x, zb, y, rows_a]

    pltpu.make_async_copy(cut(pq, me, QW), qp.at[me], recv_sems.at[R_QP]).start()
    pltpu.make_async_copy(cut(aq, me, QW), qa.at[me], recv_sems.at[R_QA]).start()
    own_parts = (
        (cut(pk, chip, DH), k_land, R_KV), (cut(pv, chip, DH), v_land, R_KV),
        (cut(ak, chip, DH), ak_land, R_AKV), (cut(av, chip, DH), av_land, R_AKV))

    @pl.when(core == mine)
    def _():
        for src, dst, r in own_parts:
            pltpu.make_async_copy(src, dst, recv_sems.at[r]).start()

    pl.semaphore_wait(barrier, len(partners))

    sends = []

    def remote(src, dst, send_sem, r, dev):
        return pltpu.make_async_remote_copy(
            src_ref=src, dst_ref=dst, send_sem=send_sem,
            recv_sem=recv_sems.at[r], device_id=dev, device_id_type=MESH)

    def send(src, dst, r, dev):
        copy = remote(src, dst, send_sems.at[len(sends)], r, dev)
        copy.start()
        sends.append(copy)

    def pass_on(ref, r, dev):
        send(ref, ref, r, dev)

    def arrived(ref, r):
        pltpu.make_async_copy(ref, ref, recv_sems.at[r]).wait()

    own_sends = [remote(src, dst, aout_sems.at[1 + i], r, sibling)
                 for i, (src, dst, r) in enumerate(own_parts)]

    def part_of(c, d1, d2, n=slice(None)):
        zz = around(zh, (1 - c) * d1 + c * d2)
        yy = around(y, (1 - c) * d2 + c * d1)
        return kv.at[n, pl.ds(2 * c, 2), zz, :, yy]

    def shard(d1, d2):
        return part_of(core, d1, d2)

    def to_sibling(d1, d2):
        k = DISTANCES.index(d2) * 4 + DISTANCES.index(d1)
        pass_on(shard(d1, d2), R_SIB + k, sibling)

    def from_sibling(d1, d2):
        k = DISTANCES.index(d2) * 4 + DISTANCES.index(d1)
        arrived(part_of(other, d1, d2), R_SIB + k)

    def start_first():
        for k, d in enumerate((1, -1, 2)):
            pass_on(shard(0, 0), R_FIRST + k, first(d))

    def start_second(d1):
        r = R_SECOND + 3 * DISTANCES.index(d1)
        pass_on(shard(d1, 0), r, second(1))
        pass_on(shard(d1, 0), r + 1, second(-1))

    def middle_second(d1):
        r = R_SECOND + 3 * DISTANCES.index(d1)
        arrived(shard(d1, -1), r)
        pass_on(part_of(core, d1, -1, 0), r + 2, second(1))
        arrived(shard(d1, 1), r + 1)
        pass_on(part_of(core, d1, 1, 1), r + 2, second(-1))
        to_sibling(d1, -1)
        to_sibling(d1, 1)

    def hand_over(d1):
        arrived(shard(d1, 2), R_SECOND + 3 * DISTANCES.index(d1) + 2)
        to_sibling(d1, 2)

    def own_keys(c, dy, n=slice(None)):
        return akv.at[n, pl.ds(2 * c, 2), :, around(y, dy)]

    for d in (7, 6, 5, 4, 3, 2, 1):
        h, xx, zz = chips[d]
        send(cut(pk, h, DH), k_land, R_KV, place(xx, zz, y, mine))
        send(cut(pv, h, DH), v_land, R_KV, place(xx, zz, y, mine))

    @pl.when(core != mine)
    def _():
        for copy in own_sends:
            copy.start()

    for d in (7, 6, 5, 4, 3, 2, 1):
        h, xx, zz = chips[d]
        send(cut(ak, h, DH), ak_land, R_AKV, place(xx, zz, y, mine))
        send(cut(av, h, DH), av_land, R_AKV, place(xx, zz, y, mine))
    arrived(shard(0, 0), R_KV)
    start_first()
    start_second(0)
    to_sibling(0, 0)
    arrived(own_keys(core, 0), R_AKV)
    pass_on(own_keys(core, 0), R_A, y_dev(1))
    pass_on(own_keys(core, 0), R_A + 1, y_dev(-1))
    pass_on(own_keys(core, 0), R_ASIB, sibling)
    for g, dev in members[:0:-1]:
        send(cut(aq, g, QW), qa.at[me], R_QA, dev)
    for k, d1 in enumerate((-1, 1, 2)):
        arrived(shard(d1, 0), R_FIRST + k)
        start_second(d1)
        to_sibling(d1, 0)
    for g, dev in members[:0:-1]:
        send(cut(pq, g, QW), qp.at[me], R_QP, dev)

    bufs = (s0, s1)

    def low(dy):
        def take(n):
            return kv[n, 0:2, :, :, around(y, dy)].reshape(512, DH)
        return (lambda: take(0), lambda: take(1), None)

    def high(dz):
        def take(n):
            return kv[n, 2:4, around(zh, dz)].reshape(512, DH)
        return (lambda: take(0), lambda: take(1), None)

    def half_slab(xx, h, mask=None):
        def take(n):
            return kv[n, xx, 2 * h:2 * h + 2].reshape(512, DH)
        return (lambda: take(0), lambda: take(1), mask)

    def iota(height, axis):
        return lax.broadcasted_iota(jnp.int32, (height, 512), axis)

    def answer_tile(t):
        return jnp.concatenate(
            [qa[4 * t + c, :, j * DH:(j + 1) * DH] for j in range(4) for c in range(4)], axis=0)

    def prompt_tile(t):
        return jnp.concatenate(
            [qp[4 * t + c, :, j * DH:(j + 1) * DH] for j in range(4) for c in range(4)], axis=0)

    def wide(b):
        return lambda i: bufs[b].at[i]

    def tall(b):
        return lambda i: bufs[b].at[i // 2, (i % 2) * 256:(i % 2) * 256 + 256]

    def keep(n, top, acc):
        tops[n] = jnp.broadcast_to(top, (512, DH))
        accs[n] = acc

    def kept(t):
        return tops[t][:, :1], accs[t]

    early = len(sends)

    for d1 in DISTANCES:
        from_sibling(d1, 0)
    arrived(qa, R_QA)
    run_items([
        Item(lambda t=t: answer_tile(t), [low(0), high(0)], wide(t % 2)) for t in range(4)
    ], keep)

    for d1 in DISTANCES:
        middle_second(d1)
    arrived(own_keys(core, -1), R_A)
    pass_on(own_keys(core, -1, 0), R_A + 2, y_dev(1))
    arrived(own_keys(core, 1), R_A + 1)
    pass_on(own_keys(core, 1, 1), R_A + 2, y_dev(-1))
    pass_on(own_keys(core, -1), R_ASIB + 1, sibling)
    pass_on(own_keys(core, 1), R_ASIB + 2, sibling)
    for copy in sends[:early]:
        copy.wait_send()
    for d2 in (-1, 1):
        for d1 in DISTANCES:
            from_sibling(d1, d2)

    def after_second(n, top, acc):
        keep(n, top, acc)
        if n == 2:
            for d1 in DISTANCES:
                hand_over(d1)
            arrived(own_keys(core, 2), R_A + 2)
            pass_on(own_keys(core, 2), R_ASIB + 3, sibling)

    run_items([
        Item(lambda t=t: answer_tile(t), [f(d) for d in (-1, 1) for f in (low, high)],
             wide(t % 2), lambda t=t: kept(t))
        for t in range(4)
    ], after_second)

    for d1 in DISTANCES:
        from_sibling(d1, 2)
    arrived(qp, R_QP)
    for dy, r in ((0, 0), (-1, 1), (1, 2), (2, 3)):
        arrived(own_keys(other, dy), R_ASIB + r)

    def prompt_mask(h):
        rows = iota(256, 0)
        here = (2 * zh) * 128 + y * 32 + ((rows // 32) % 2) * 128 + rows % 32
        return iota(256, 1) + h * 512 <= here

    def answer_mask():
        rows = iota(512, 0)
        return iota(512, 1) <= ((rows // 64) % 2) * 256 + y * 64 + rows % 64

    prompt_order = (3, 2, 1, 0)
    answer_order = (2, 1, 3, 0)
    last_items = []
    for dx in answer_order:
        t = (x + dx) % 4
        own_piece = (
            lambda t=t: akv[0, t].reshape(512, DH), lambda t=t: akv[1, t].reshape(512, DH),
            answer_mask)
        last_items.append(Item(
            lambda t=t: answer_tile(t), [low(2), high(2), own_piece], wide((0, 1, 0, 1)[len(last_items)]),
            lambda t=t: kept(t)))
    for t in prompt_order:
        pieces = [half_slab(i, h) for i in range(t) for h in range(2)]
        pieces += [half_slab(t, h, lambda h=h: prompt_mask(h)) for h in range(2)]
        last_items.append(Item(lambda t=t: prompt_tile(t), pieces, tall((len(last_items) + 1) % 2)))

    last_items.append(last_items.pop(3))

    def finished(acc):
        return (acc[:, :DH] / acc[:, DH:]).astype(jnp.bfloat16)

    def after_last(n, top, acc):
        if 3 <= n < 7:
            t = prompt_order[n - 3]
            out = finished(acc)
            for j in range(4):
                for c in range(4):
                    r = j * 64 + c * 16
                    op[4 * t + c, :, j * DH:(j + 1) * DH] = out[r:r + 16]
            for c in range(4):
                g = 4 * t + c
                dst = cut(po, me, QW)

                @pl.when(g != me)
                def _(g=g, c=c, dst=dst):
                    remote(op.at[g], dst, pout_sems.at[0], R_OP,
                           place(t, zh * 2 + c // 2, y, c % 2)).start()

                @pl.when(g == me)
                def _(g=g, dst=dst):
                    pltpu.make_async_copy(op.at[g], dst, recv_sems.at[R_OP]).start()
            return
        dx = answer_order[min(n, 3)]
        t = (x + dx) % 4
        out = finished(acc)
        for j in range(4):
            for c in range(4):
                r = j * 128 + c * 32
                oa[4 * t + c, :, j * DH:(j + 1) * DH] = out[r:r + 32]
        dst = cut(ao, me, QW)
        for k in (3, 2, 1, 0):
            d = dx * 4 + k
            g, dev = members[d]
            if d:
                remote(oa.at[g], dst, aout_sems.at[0], R_OA, dev).start()
            else:
                pltpu.make_async_copy(oa.at[g], dst, recv_sems.at[R_OA]).start()

    run_items(last_items, after_last)

    assert len(sends) <= N_SEND
    for copy in sends[early:]:
        copy.wait_send()

    @pl.when(core != mine)
    def _():
        for copy in own_sends:
            copy.wait_send()

    pltpu.make_async_copy(op.at[0:15], op.at[0:15], pout_sems.at[0]).wait()
    pltpu.make_async_copy(oa.at[0:15], oa.at[0:15], aout_sems.at[0]).wait()
    arrived(po, R_OP)
    arrived(ao, R_OA)


def closing(lengths, prompt_in, answer_in, prompt_out, answer_out):
    seq, resp = lax.axis_index("seq"), lax.axis_index("resp")
    height = answer_in.shape[0]
    live = lengths[seq // 2] - (seq % 2) * 256 - resp * height
    prompt_out[...] = prompt_in[...]
    for i in range(0, answer_in.shape[1], 1024):
        rows = lax.broadcasted_iota(jnp.int32, (height, 1024), 0)
        values = answer_in[:, i:i + 1024].astype(jnp.float32)
        answer_out[:, i:i + 1024] = jnp.where(rows < live, values, 0.0).astype(jnp.bfloat16)


def shards(pq, pk, pv, aq, ak, av, answer_lengths):
    bf16, f32 = jnp.bfloat16, jnp.float32
    any_spec = pl.BlockSpec(memory_space=pl.ANY)
    prompt_out, answer_out = pl.pallas_call(
        kernel,
        out_shape=(
            jax.ShapeDtypeStruct(pq.shape, bf16),
            jax.ShapeDtypeStruct(aq.shape, bf16),
        ),
        in_specs=[any_spec] * 6,
        out_specs=(any_spec, any_spec),
        scratch_shapes=[
            pltpu.VMEM((2, 4, 4, 2, 4, 32, DH), bf16),
            pltpu.VMEM((2, 4, 2, 4, 64, DH), bf16),
            pltpu.VMEM((16, 16, QW), bf16),
            pltpu.VMEM((16, 32, QW), bf16),
            pltpu.VMEM((16, 16, QW), bf16),
            pltpu.VMEM((16, 32, QW), bf16),
            pltpu.VMEM((4, 512, 2 * DH), f32),
            pltpu.VMEM((4, 512, DH), f32),
            pltpu.VMEM((6, 512, 512), f32),
            pltpu.VMEM((6, 512, 512), f32),
            pltpu.SemaphoreType.DMA((N_SEND,)),
            pltpu.SemaphoreType.DMA((1,)),
            pltpu.SemaphoreType.DMA((5,)),
            pltpu.SemaphoreType.DMA((N_RECV,)),
        ],
        compiler_params=pltpu.CompilerParams(
            collective_id=0, has_side_effects=True, vmem_limit_bytes=60 * 1024 * 1024),
        cost_estimate=pl.CostEstimate(
            flops=6_400_000_000, bytes_accessed=2_000_000, transcendentals=12_000_000),
    )(pq, pk, pv, aq, ak, av)
    vmem = pl.BlockSpec(memory_space=pltpu.VMEM)
    return pl.pallas_call(
        closing,
        out_shape=(
            jax.ShapeDtypeStruct(pq.shape, bf16),
            jax.ShapeDtypeStruct(aq.shape, bf16),
        ),
        in_specs=[pl.BlockSpec(memory_space=pltpu.SMEM), vmem, vmem],
        out_specs=(vmem, vmem),
        name="closing",
    )(answer_lengths, prompt_out, answer_out)


def solution(mesh):
    rows = P(("prompt", "seq", "resp"), None)
    return jax.shard_map(
        shards,
        mesh=mesh,
        in_specs=(rows,) * 6 + (P("prompt"),),
        out_specs=(rows, rows),
        check_vma=False,
    )
```
